256 devices in a mesh: dp: 64 (over z, x, core), tensor: 4 (over y).
Axes of the slice: x: 4, y: 4, z: 8, core: 2. Of those that a mesh axis runs over, the one named last changes fastest.
Arguments:
- activations: bfloat16 [896, 8192], P('dp', 'tensor'), may hold values from -6 to 6
- gate_weight: bfloat16 [8192, 28672], P(None, ('dp', 'tensor')), may hold values from -0.0625 to 0.0625
- up_weight: bfloat16 [8192, 28672], P(None, ('dp', 'tensor')), may hold values from -0.0625 to 0.0625
- anchor_states: bfloat16 [80, 28672], P(None, ('dp', 'tensor')), may hold values from -6 to 6
- token_ids: int32 [896], replicated, may hold values from 0 to 128255
- anchor_layer: int32 [896], replicated, may hold values from 0 to 79
- token_weight: float32 [128256], replicated, may hold values from 0.3 to 3
Outputs:
- act_covariance: float32 [8192, 8192], P('dp', 'tensor')
- grad_covariance: bfloat16 [28672, 28672], P('dp', 'tensor')
The draws below stay inside these ranges and needn't reach their ends.
All inputs are finite; a program needn't handle non-finite values.
Results may differ from the reference program's by a relative error of at most 0.0053.
Values may be sent and summed in bfloat16 or wider, within the bound.
No kernel may reach another device: no remote copies, remote signals or barrier semaphores. Data moves between devices by JAX's collectives and lax.ppermute only.
A program may use at most 128 MiB of HBM per device.

```python
import math
import jax
import jax.numpy as jnp
import numpy as np
from jax import lax

D = 8192
FF = 28672
VOCAB = 128256
NANCH = 80
TOKENS = 896
N_DP = 64
N_TENSOR = 4


def plant(entries, rng, low, largest):
    longest = entries.shape.index(max(entries.shape))
    spots = []
    for shift in (0, 1):
        where = [jax.random.randint(jax.random.fold_in(rng, axis), (), 0, length) for axis, length in enumerate(entries.shape)]
        where[longest] = (where[longest] + shift) % entries.shape[longest]
        spots.append(tuple(where))
    return entries.at[spots[0]].set(low).at[spots[1]].set(largest)


def levels(own_key, extent, pieces, low, top_value):
    def one(axis_at, blocks):
        draws = jax.random.uniform(jax.random.fold_in(jax.random.fold_in(own_key, 6), axis_at), (blocks,), jnp.float32, low / len(pieces), top_value / len(pieces))
        return jnp.repeat(jnp.exp(draws), extent[axis_at] // blocks).reshape((-1,) + (1,) * (len(extent) - axis_at - 1))

    factor_of = one(*pieces[0])
    for cut in pieces[1:]:
        factor_of = factor_of * one(*cut)
    return factor_of


def skewed_wide(rng, dims, count, lean):
    weights = [min(1 << octave, count + 1 - (1 << octave)) * (1 << 20) // math.isqrt((1 << octave) ** lean) + 1 for octave in range((count + 1).bit_length()) if 1 << octave <= count]
    deviation = 1 + sum(weights) // (1 << 30)
    listing = np.cumsum(np.array([max(1, weight // deviation) for weight in weights]))
    lot = jax.random.randint(jax.random.fold_in(rng, 1), dims, 0, int(listing[len(weights) - 1]))
    start = jnp.left_shift(1, jnp.searchsorted(jnp.asarray(listing, jnp.int32), lot, side="right").astype(jnp.int32))
    rank = start - 1 + jax.random.randint(jax.random.fold_in(rng, 4), dims, 0, 1 << 30) % jnp.minimum(start, count + 1 - start)
    return jax.random.permutation(jax.random.fold_in(rng, 2), count)[rank].astype(jnp.int32)


def centred(stream_key, dims, scale, most, pieces=(), held_as=jnp.bfloat16):
    array = jax.random.normal(stream_key, dims, jnp.float32) * scale
    if len(pieces) > 0:
        array = levels(stream_key, dims, pieces, -0.22, 0.18) * array
    return jnp.clip(array, min=-most, max=most).astype(held_as)


def setup_inputs(seed: int = 0) -> dict:
    splits = jax.random.split(jax.random.key(seed), 8)
    return {
        "activations": centred(splits[0], (TOKENS, D), 1.0, 6.0, ((0, 64), (1, 4))),
        "gate_weight": centred(splits[1], (D, FF), D ** -0.5, 0.0625, ((1, 256),)),
        "up_weight": centred(splits[2], (D, FF), D ** -0.5, 0.0625, ((1, 256),)),
        "anchor_states": centred(splits[3], (NANCH, FF), 1.0, 6.0, ((1, 256),)),
        "token_ids": plant(skewed_wide(splits[4], (TOKENS,), VOCAB, 2), jax.random.fold_in(splits[4], 3), 0, VOCAB - 1).astype(jnp.int32),
        "anchor_layer": plant(jax.random.randint(splits[5], (TOKENS,), 0, NANCH), jax.random.fold_in(splits[5], 1), 0, NANCH - 1).astype(jnp.int32),
        "token_weight": jnp.clip(jnp.exp(jax.random.uniform(splits[6], (VOCAB,), jnp.float32, math.log(0.3), math.log(3.0))), 0.3, 3.0),
    }


def reference(activations, gate_weight, up_weight, anchor_states, token_ids, anchor_layer, token_weight):
    gate = jnp.dot(activations, gate_weight, preferred_element_type=jnp.float32)
    up = jnp.dot(activations, up_weight, preferred_element_type=jnp.float32)
    sig = jax.nn.sigmoid(gate)
    hidden = gate * sig * up
    target = anchor_states[anchor_layer].astype(jnp.float32)
    scale = token_weight[token_ids]
    loss_grad = scale[:, None] * (hidden - target)
    grad_gate = (loss_grad * up * sig * (1.0 + gate * (1.0 - sig))).astype(jnp.bfloat16)
    act_covariance = lax.dot_general(activations, activations, (((0,), (0,)), ((), ())), preferred_element_type=jnp.float32) / TOKENS
    per_unit = FF // (N_DP * N_TENSOR)
    ordered = grad_gate.reshape(TOKENS, N_DP, N_TENSOR, per_unit).transpose(0, 2, 1, 3).reshape(TOKENS, FF)
    row_blocks = grad_gate.reshape(TOKENS, N_DP, FF // N_DP).transpose(1, 0, 2)

    def one_block(block):
        prod = lax.dot_general(block, ordered, (((0,), (0,)), ((), ())), preferred_element_type=jnp.float32)
        return (prod / TOKENS).astype(jnp.bfloat16)

    grad_covariance = lax.map(one_block, row_blocks).reshape(FF, FF)
    return act_covariance, grad_covariance
```

```python
import functools

import jax
import jax.numpy as jnp
from jax import lax
from jax.experimental import pallas as pl
from jax.experimental.pallas import tpu as pltpu
from jax.sharding import Mesh, PartitionSpec as P

NZ, NX, NC, NY = 8, 4, 2, 4
OFF4 = (0, 3, 1, 2)
F32, BF16 = jnp.float32, jnp.bfloat16


def shift(x, axis, size, step):
    return lax.ppermute(x, axis, [(i, (i + step) % size) for i in range(size)])


def swap_core(x):
    return lax.ppermute(x, "core", [(0, 1), (1, 0)])


def ring(x, axis, size, half):
    found = {0: x}
    left = right = x
    for hop in range(1, size // 2):
        left = shift(left, axis, size, 1)
        right = shift(right, axis, size, -1)
        found[size - hop] = left
        found[hop] = right
    found[size // 2] = (
        shift(left[:half], axis, size, 1),
        shift(right[half:], axis, size, -1),
    )
    return found


def flat(found, order):
    parts = []
    for off in order:
        block = found[off]
        parts += list(block) if isinstance(block, tuple) else [block]
    return parts


NT = (((1,), (1,)), ((), ()))


def whole(*shape):
    return pl.BlockSpec(shape, lambda *_: (0,) * len(shape))


def pack_kernel(where, gate, up, sib, out):
    out[...] = jnp.zeros_like(out)
    out[0, 0:112, :] = gate[...]
    out[0, 128:240, :] = up[...]
    out[0, 256:368, :] = sib[0:112, :]
    out[0, 384:496, :] = sib[112:224, :]


def pack_weights(where, gate_t, up_t, sib):
    return pl.pallas_call(
        pack_kernel,
        out_shape=jax.ShapeDtypeStruct((16, 512, 256), BF16),
        grid_spec=pltpu.PrefetchScalarGridSpec(
            num_scalar_prefetch=1,
            grid=(16,),
            in_specs=[
                pl.BlockSpec((112, 256), lambda k, w: (0, w[k] * 2 + w[16])),
                pl.BlockSpec((112, 256), lambda k, w: (0, w[k] * 2 + w[16])),
                pl.BlockSpec((224, 256), lambda k, w: (0, w[k])),
            ],
            out_specs=pl.BlockSpec((1, 512, 256), lambda k, w: (k, 0, 0)),
        ),
        name="pack_weights",
    )(where, gate_t, up_t, sib)


def product_kernel(*refs):
    a_refs, b_refs, w, own, sib = refs[0:5], refs[5:10], refs[10], refs[11], refs[12]
    for first, group, flip in ((0, a_refs, False), (448, b_refs, True)):
        rows = slice(first, first + 448)
        count = 0
        for number, ref in enumerate(group):
            major = min(number, 3)
            for i in range(ref.shape[0]):
                minor = i + (2 if number == 4 else 0)
                k = minor * 4 + major if flip else major * 4 + minor
                part = lax.dot_general(ref[i], w[k], NT, preferred_element_type=F32)
                if count == 0:
                    own[rows, :] = part[:, :256]
                    sib[rows, :] = part[:, 256:]
                else:
                    own[rows, :] += part[:, :256]
                    sib[rows, :] += part[:, 256:]
                count += 1


def product(a_parts, b_parts, w):
    out = jax.ShapeDtypeStruct((896, 256), F32)
    return pl.pallas_call(
        product_kernel,
        out_shape=(out, out),
        compiler_params=pltpu.CompilerParams(vmem_limit_bytes=40 << 20),
        name="product",
    )(*a_parts, *b_parts, w)


def gradient_kernel(own, other, target, scale, out):
    both = own[...] + other[...]
    gate, up = both[:, :128], both[:, 128:]
    sig = jax.nn.sigmoid(gate)
    hidden = gate * sig * up
    loss_grad = scale[...] * (hidden - target[...].astype(F32))
    grad = loss_grad * up * sig * (1.0 + gate * (1.0 - sig))
    out[...] = jnp.transpose(grad)[:112, :].astype(BF16)


def gradient(own, other, target, scale):
    return pl.pallas_call(
        gradient_kernel,
        out_shape=jax.ShapeDtypeStruct((112, 896), BF16),
        compiler_params=pltpu.CompilerParams(vmem_limit_bytes=24 << 20),
        name="gradient",
    )(own, other, target, scale)


def pick_kernel(where, *refs):
    a_refs, b_refs, out = refs[0:5], refs[5:10], refs[10]
    for e in range(4):
        out[e, 0:448, :] = a_refs[0][e]
        src = b_refs[e][0]
        out[e, 448:896, :] = src
    for p in range(4):
        for e in range(4):

            @pl.when(where[17] == p * 4 + e)
            def _():
                a_ref = a_refs[p + (1 if p == 3 and e >= 2 else 0)]
                b_ref = b_refs[e + (1 if e == 3 and p >= 2 else 0)]
                out[4, 0:448, :] = a_ref[e - (2 if p == 3 and e >= 2 else 0)]
                out[4, 448:896, :] = b_ref[p - (2 if e == 3 and p >= 2 else 0)]


def pick(where, a_parts, b_parts):
    return pl.pallas_call(
        pick_kernel,
        out_shape=jax.ShapeDtypeStruct((5, 896, 256), BF16),
        in_specs=[pl.BlockSpec(memory_space=pltpu.SMEM)]
        + [pl.BlockSpec(memory_space=pltpu.VMEM)] * 10,
        compiler_params=pltpu.CompilerParams(vmem_limit_bytes=40 << 20),
        name="pick",
    )(where, *a_parts, *b_parts)


def covariance_kernel(where, mine, other, mine_left, other_left, out, left):
    step = pl.program_id(0)

    @pl.when(step == 0)
    def _():
        keep = where[18] == where[16]
        both = jnp.where(keep, mine_left[0], other_left[0]).astype(F32)
        side = jnp.where(where[16] == 0, both[:, :128], both[:, 128:])
        left[...] = jnp.transpose(side).astype(BF16)

    right = jnp.where(step % 2 == 0, mine[0], other[0])
    tile = lax.dot_general(
        left[...], right, (((1,), (0,)), ((), ())), preferred_element_type=F32
    )
    out[...] = tile * (1.0 / 896.0)


def covariance(where, mine, other):
    chunk = (1, 896, 256)
    return pl.pallas_call(
        covariance_kernel,
        out_shape=jax.ShapeDtypeStruct((128, 2048), F32),
        grid_spec=pltpu.PrefetchScalarGridSpec(
            num_scalar_prefetch=1,
            grid=(8,),
            in_specs=[
                pl.BlockSpec(chunk, lambda s, w: (s // 2, 0, 0)),
                pl.BlockSpec(chunk, lambda s, w: (s // 2, 0, 0)),
                pl.BlockSpec(chunk, lambda s, w: (4, 0, 0)),
                pl.BlockSpec(chunk, lambda s, w: (4, 0, 0)),
            ],
            out_specs=pl.BlockSpec(
                (128, 256), lambda s, w: (0, w[19 + s // 2] * 2 + (w[16] + s % 2) % 2)
            ),
            scratch_shapes=[pltpu.VMEM((128, 896), BF16)],
        ),
        compiler_params=pltpu.CompilerParams(vmem_limit_bytes=24 << 20),
        name="covariance",
    )(where, mine, other, mine, other)


def tile_kernel(where, *refs):
    rows, refs = refs[0:5], refs[5:]
    z_mine, z_other, refs = refs[0:9], refs[9:18], refs[18:]
    x_mine, x_other = refs[0:5], refs[5:10]
    out, left, right = refs[10:13]
    step = pl.program_id(0)
    core = where[16]

    @pl.when(step == 0)
    def _():
        for number, ref in enumerate(rows):
            base = where[23 + min(number, 3)] * 112 + (48 if number == 4 else 0)
            left[pl.ds(pl.multiple_of(base, 16), ref.shape[0]), :] = ref[...]

    for number in range(8):

        @pl.when(step == number)
        def _():
            for e in range(4):
                for z_refs, x_refs, who in ((z_mine, x_mine, core), (z_other, x_other, 1 - core)):
                    base = (where[19 + e] * 2 + who) * 112
                    if number < 7:
                        block = z_refs[number][e * 64 : e * 64 + 64, :]
                    else:
                        block = z_refs[7 + e // 2][(e % 2) * 64 : (e % 2) * 64 + 64, :]
                    right[pl.ds(pl.multiple_of(base, 16), 64), :] = block
                    if e < 3:
                        more = x_refs[e][number * 48 : number * 48 + 48, :]
                    else:
                        more = x_refs[3 + number // 4][(number % 4) * 48 : (number % 4) * 48 + 48, :]
                    right[pl.ds(pl.multiple_of(base + 64, 16), 48), :] = more

    tile = lax.dot_general(left[...], right[...], NT, preferred_element_type=F32)
    out[...] = (tile * (1.0 / 896.0)).astype(BF16)


def tile(where, parts):
    return pl.pallas_call(
        tile_kernel,
        out_shape=jax.ShapeDtypeStruct((448, 7168), BF16),
        grid_spec=pltpu.PrefetchScalarGridSpec(
            num_scalar_prefetch=1,
            grid=(8,),
            in_specs=[whole(*part.shape) for part in parts],
            out_specs=pl.BlockSpec((448, 896), lambda s, w: (0, w[27 + s])),
            scratch_shapes=[pltpu.VMEM((448, 896), BF16), pltpu.VMEM((896, 896), BF16)],
        ),
        compiler_params=pltpu.CompilerParams(vmem_limit_bytes=56 << 20),
        name="tile",
    )(where, *parts)


OFF8 = (0, 7, 1, 6, 2, 5, 3, 4)


def body(activations, gate_weight, up_weight, anchor_states, token_ids, anchor_layer, token_weight):
    z, x = lax.axis_index("z"), lax.axis_index("x")
    core, y = lax.axis_index("core"), lax.axis_index("y")

    def around(me, size, offs):
        return [(me + off) % size for off in offs]

    xs, ys, zs = around(x, NX, OFF4), around(y, NY, OFF4), around(z, NZ, OFF8)
    left_y, left_x, left_core = z // 2, (z % 2) * 2 + x // 2, x % 2
    place = sum((((ys[p] == left_y) & (xs[e] == left_x)) * (p * 4 + e) for p in range(4) for e in range(4)))
    table = [ys[p] * 4 + xs[e] for p in range(4) for e in range(4)]
    table += [core, place, left_core] + xs + ys + zs
    where = jnp.stack([jnp.asarray(v, jnp.int32) for v in table])

    chunks = activations.reshape(14, 8, 256).transpose(1, 0, 2)
    chunk = lax.all_to_all(chunks, ("x", "core"), 0, 0).reshape(112, 256)

    gate_t, up_t = gate_weight.T, up_weight.T
    halves = jnp.concatenate([gate_t, up_t], 0).reshape(224, 16, 2, 256)
    away = lax.dynamic_index_in_dim(halves, 1 - core, 2, keepdims=False).reshape(224, 4096)
    weights = pack_weights(where, gate_t, up_t, swap_core(away))

    found = ring(chunk, "z", NZ, 48)
    line = jnp.concatenate(flat(found, range(8)), 0)
    line = lax.dynamic_slice_in_dim(
        jnp.concatenate([line, line], 0), (NZ - z) % NZ * 112, 896, 0
    )

    def two_rings(block, axes):
        size = 448
        near = ring(block, axes[0], 4, size // 2)
        near = jnp.concatenate(flat(near, OFF4), 0).reshape(4, size, 256)
        return flat(ring(near, axes[1], 4, 2), OFF4)

    a_parts = two_rings(line[:448], ("x", "y"))
    b_parts = two_rings(line[448:], ("y", "x"))

    padded = jnp.pad(anchor_states, ((0, 0), (0, 16)))
    target = padded[anchor_layer]
    scale = token_weight[token_ids][:, None]

    own, sib = product(a_parts, b_parts, weights)
    grads = gradient(own, swap_core(sib), target, scale)

    rows = flat(ring(grads, "y", NY, 48), OFF4)
    by_x = jnp.concatenate(flat(ring(grads[:64], "x", NX, 32), OFF4), 0)
    by_z = jnp.concatenate(flat(ring(grads[64:], "z", NZ, 16), OFF8), 0)
    z_mine = flat(ring(by_x, "z", NZ, 128), OFF8)
    x_mine = flat(ring(by_z, "x", NX, 192), OFF4)
    z_other = [swap_core(part) for part in z_mine]
    x_other = [swap_core(part) for part in x_mine]

    mine = pick(where, a_parts, b_parts)
    act_covariance = covariance(where, mine, swap_core(mine))
    grad_covariance = tile(where, rows + z_mine + z_other + x_mine + x_other)
    return act_covariance, grad_covariance


def solution(mesh):
    fine = Mesh(mesh.devices.reshape(NZ, NX, NC, NY), ("z", "x", "core", "y"))
    dp = ("z", "x", "core")
    units = P(None, dp + ("y",))
    in_specs = (P(dp, "y"), units, units, units, P(), P(), P())
    out_specs = (P(dp, "y"), P(dp, "y"))
    return jax.shard_map(body, mesh=fine, in_specs=in_specs, out_specs=out_specs, check_vma=False)
```

```python
import functools

import jax
import jax.numpy as jnp
from jax import lax
from jax.experimental import pallas as pl
from jax.experimental.pallas import tpu as pltpu
from jax.sharding import Mesh, PartitionSpec as P

NZ, NX, NC, NY = 8, 4, 2, 4
OFF4 = (0, 3, 1, 2)
F32, BF16 = jnp.float32, jnp.bfloat16


def shift(x, axis, size, step):
    return lax.ppermute(x, axis, [(i, (i + step) % size) for i in range(size)])


def swap_core(x):
    return lax.ppermute(x, "core", [(0, 1), (1, 0)])


def pair_step(x, axis, hop):
    size = {"x": NX, "z": NZ}[axis]
    perm = [(i * 2 + c, (i + s) % size * 2 + c) for c, s in ((0, hop), (1, -hop)) for i in range(size)]
    return lax.ppermute(x, (axis, "core"), perm)


def direct(x, axis):
    return [x] + [shift(x, axis, 4, step) for step in (1, -1, 2)]


def ring(x, axis, size, half):
    found = {0: x}
    left = right = x
    for hop in range(1, size // 2):
        left = shift(left, axis, size, 1)
        right = shift(right, axis, size, -1)
        found[size - hop] = left
        found[hop] = right
    found[size // 2] = (
        shift(left[:half], axis, size, 1),
        shift(right[half:], axis, size, -1),
    )
    return found


def flat(found, order):
    parts = []
    for off in order:
        block = found[off]
        parts += list(block) if isinstance(block, tuple) else [block]
    return parts


NT = (((1,), (1,)), ((), ()))
SCALARS = pl.BlockSpec(memory_space=pltpu.SMEM)


def params(mib):
    return pltpu.CompilerParams(vmem_limit_bytes=mib << 20)


def cost(mib, gflop=0):
    return pl.CostEstimate(flops=gflop << 30, bytes_accessed=mib << 20, transcendentals=0)


def whole(*shape):
    return pl.BlockSpec(shape, lambda *_: (0,) * len(shape))


def join_kernel(pieces, *refs):
    out = refs[-1]
    at = 0
    for number, first, count in pieces:
        out[at : at + count] = refs[number][first : first + count]
        at += count


def join(pieces):
    arrays, plan = [], []
    for array, first, count in pieces:
        number = next((i for i, seen in enumerate(arrays) if seen is array), len(arrays))
        if number == len(arrays):
            arrays.append(array)
        plan.append((number, first, count))
    rows = sum(count for _, _, count in plan)
    return pl.pallas_call(
        functools.partial(join_kernel, plan),
        out_shape=jax.ShapeDtypeStruct((rows,) + arrays[0].shape[1:], BF16),
        compiler_params=params(8),
        cost_estimate=cost(2),
        name="join",
    )(*arrays)


def lineup_kernel(where, mine, one, two, three, turned, far, out):
    lanes = pl.ds(pl.multiple_of(where[16] * 1024, 1024), 1024)
    out[where[27]] = mine[...]
    for number, ref in enumerate((one, two, three)):
        out[where[28 + number]] = ref[:, lanes]
        out[where[31 + number]] = turned[number]
    out[where[34]] = far[...]


def lineup(where, *blocks):
    return pl.pallas_call(
        lineup_kernel,
        out_shape=jax.ShapeDtypeStruct((8, 28, 1024), BF16),
        in_specs=[SCALARS] + [whole(*block.shape) for block in blocks],
        compiler_params=params(6),
        name="lineup",
    )(where, *blocks)


def away_kernel(where, gate, up, out):
    for part in range(4):
        lanes = pl.ds(pl.multiple_of(part * 2048 + (1 - where[16]) * 1024, 1024), 1024)
        out[part, 0:112, :] = gate[:, lanes]
        out[part, 112:224, :] = up[:, lanes]


def away_half(where, gate_t, up_t):
    return pl.pallas_call(
        away_kernel,
        out_shape=jax.ShapeDtypeStruct((4, 224, 1024), BF16),
        in_specs=[SCALARS, whole(*gate_t.shape), whole(*up_t.shape)],
        compiler_params=params(10),
        cost_estimate=cost(6),
        name="away_half",
    )(where, gate_t, up_t)


def pack_kernel(where, gate, up, sib, out):
    blank = jnp.zeros((16, 1024), BF16)
    for k in range(4):
        part = where[23 + k]
        lanes = pl.ds(pl.multiple_of(part * 2048 + where[16] * 1024, 1024), 1024)
        pieces = (gate[:, lanes], up[:, lanes], sib[part, 0:112, :], sib[part, 112:224, :])
        for number, piece in enumerate(pieces):
            out[k, number * 128 : number * 128 + 112, :] = piece
            out[k, number * 128 + 112 : number * 128 + 128, :] = blank


def pack_weights(where, gate_t, up_t, sib):
    return pl.pallas_call(
        pack_kernel,
        out_shape=jax.ShapeDtypeStruct((4, 512, 1024), BF16),
        in_specs=[SCALARS, whole(*gate_t.shape), whole(*up_t.shape), whole(*sib.shape)],
        compiler_params=params(14),
        cost_estimate=cost(12),
        name="pack_weights",
    )(where, gate_t, up_t, sib)


def near_kernel(a0, a1, a2, b0, b1, b2, w, own, sib):
    for p, ref in enumerate((a0, a1, a2)):
        block = ref[...].reshape(896, 512)
        part = lax.dot_general(block, w[p, :, 0:512], NT, preferred_element_type=F32)
        if p == 0:
            own[...] = part[:, :256]
            sib[...] = part[:, 256:]
        else:
            own[...] += part[:, :256]
            sib[...] += part[:, 256:]
    for e, ref in enumerate((b0, b1, b2)):
        rows = slice(e * 224, e * 224 + 224)
        for p in range(4):
            part = lax.dot_general(ref[p], w[p, :, 512:1024], NT, preferred_element_type=F32)
            own[rows, :] += part[:, :256]
            sib[rows, :] += part[:, 256:]


def near_product(a_parts, b_parts, w):
    out = jax.ShapeDtypeStruct((896, 256), F32)
    return pl.pallas_call(
        near_kernel,
        out_shape=(out, out),
        compiler_params=params(22),
        cost_estimate=cost(12, 3),
        name="near_product",
    )(*a_parts, *b_parts, w)


def far_kernel(where, a_low, a_high, b_low, b_high, w, own_in, sib_in, own, sib):
    for e in range(4):
        at = slice(e * 224, e * 224 + 224)
        rows = pl.ds(pl.multiple_of(where[43 + e] * 224, 16), 224)
        block = (a_low, a_high)[e // 2][e % 2]
        part = lax.dot_general(block, w[3, :, 0:512], NT, preferred_element_type=F32)
        if e == 3:
            for p in range(4):
                more = (b_low, b_high)[p // 2][p % 2]
                part += lax.dot_general(more, w[p, :, 512:1024], NT, preferred_element_type=F32)
        own[rows, :] = own_in[at, :] + part[:, :256]
        sib[rows, :] = sib_in[at, :] + part[:, 256:]


def far_product(where, a_parts, b_parts, w, own, sib):
    out = jax.ShapeDtypeStruct((896, 256), F32)
    operands = (*a_parts, *b_parts, w, own, sib)
    return pl.pallas_call(
        far_kernel,
        out_shape=(out, out),
        in_specs=[SCALARS] + [whole(*operand.shape) for operand in operands],
        compiler_params=params(18),
        cost_estimate=cost(8, 1),
        name="far_product",
    )(where, *operands)


def gradient_kernel(own, other, target, scale, out):
    both = own[...] + other[...]
    gate, up = both[:, :128], both[:, 128:]
    sig = jax.nn.sigmoid(gate)
    hidden = gate * sig * up
    loss_grad = scale[...] * (hidden - target[...].astype(F32))
    grad = loss_grad * up * sig * (1.0 + gate * (1.0 - sig))
    out[...] = jnp.transpose(grad)[:112, :].astype(BF16)


def gradient(own, other, target, scale):
    return pl.pallas_call(
        gradient_kernel,
        out_shape=jax.ShapeDtypeStruct((112, 896), BF16),
        compiler_params=params(10),
        name="gradient",
    )(own, other, target, scale)


def pick_kernel(where, *refs):
    a_refs, b_refs, out = refs[0:5], refs[5:10], refs[10]
    x = where[43]

    def rows(e):
        return pl.ds(pl.multiple_of(where[43 + e] * 224, 16), 224)

    for e in range(4):
        out[rows(e), 0:512] = a_refs[0][e]
        out[rows(e), 512:1024] = b_refs[e][0]
    lanes = pl.ds(pl.multiple_of(x % 2 * 256, 256), 256)
    for p in range(4):

        @pl.when((where[17] == p) & (x < 2))
        def _():
            for e in range(4):
                ref, row = (a_refs[p], e) if p < 3 else (a_refs[3 + e // 2], e % 2)
                out[rows(e), 1024:1280] = ref[row, :, lanes]

        @pl.when((where[17] == p) & (x >= 2))
        def _():
            for e in range(4):
                ref, row = (b_refs[e], p) if e < 3 else (b_refs[3 + p // 2], p % 2)
                out[rows(e), 1024:1280] = ref[row, :, lanes]


def pick(where, a_parts, b_parts):
    operands = (*a_parts, *b_parts)
    return pl.pallas_call(
        pick_kernel,
        out_shape=jax.ShapeDtypeStruct((896, 1280), BF16),
        in_specs=[SCALARS] + [whole(*operand.shape) for operand in operands],
        compiler_params=params(14),
        cost_estimate=cost(12),
        name="pick",
    )(where, *operands)


def covariance_kernel(where, mine, other, mine_left, other_left, out, left):
    step = pl.program_id(0)

    @pl.when(step == 0)
    def _():
        keep = where[18] == where[16]
        both = jnp.where(keep, mine_left[...], other_left[...]).astype(F32)
        side = jnp.where(where[16] == 0, both[:, :128], both[:, 128:])
        left[...] = jnp.transpose(side).astype(BF16)

    right = jnp.where(step % 2 == 0, mine[...], other[...])
    tile = lax.dot_general(
        left[...], right, (((1,), (0,)), ((), ())), preferred_element_type=F32
    )
    out[...] = tile * (1.0 / 896.0)


def covariance(where, mine, other):
    chunk = (896, 256)
    return pl.pallas_call(
        covariance_kernel,
        out_shape=jax.ShapeDtypeStruct((128, 2048), F32),
        grid_spec=pltpu.PrefetchScalarGridSpec(
            num_scalar_prefetch=1,
            grid=(8,),
            in_specs=[
                pl.BlockSpec(chunk, lambda s, w: (0, s // 2)),
                pl.BlockSpec(chunk, lambda s, w: (0, s // 2)),
                pl.BlockSpec(chunk, lambda s, w: (0, 4)),
                pl.BlockSpec(chunk, lambda s, w: (0, 4)),
            ],
            out_specs=pl.BlockSpec(
                (128, 256), lambda s, w: (0, s // 2 + 4 * ((w[16] + s % 2) % 2))
            ),
            scratch_shapes=[pltpu.VMEM((128, 896), BF16)],
        ),
        compiler_params=params(8),
        cost_estimate=cost(8, 1),
        name="covariance",
    )(where, mine, other, mine, other)


UA, UB = 64, 48
TURN = (0, 4, 5, 6, 1, 2, 3, 7)
EARLY, LATE = (0, 1, 2, 4, 5), (3, 6, 7)


def tile_kernel(numbers, where, *refs):
    rows, refs = refs[0:5], refs[5:]
    count = sum(2 if number == 7 else 1 for number in numbers)
    a_refs, refs = refs[0:count], refs[count:]
    (x0, x0b, xd, xdb, xs, xsb, xf, xfb) = refs[0:8]
    out, left, right = refs[-3:]
    step = pl.program_id(0)
    core = where[16]

    def put(slot_x, who, first, value):
        base = (where[19 + slot_x] * 2 + who) * 112 + first
        right[pl.ds(pl.multiple_of(base, 16), value.shape[0]), :] = value

    @pl.when(step == 0)
    def _():
        for number, ref in enumerate(rows):
            base = where[23 + min(number, 3)] * 112 + (48 if number == 4 else 0)
            left[pl.ds(pl.multiple_of(base, 16), ref.shape[0]), :] = ref[...]

    for at, number in enumerate(numbers):

        @pl.when(step == at)
        def _():
            for e in range(4):
                mirror = (0, 2, 1, 3)[e]
                for half in range(2):
                    ref = a_refs[at]
                    if number < 4:
                        who, place = (core, 1 - core)[half], half * 4 + e
                    elif number < 7:
                        who, place = (1 - core, core)[half], half * 4 + mirror
                    elif half == 0:
                        who, place = core, e
                    else:
                        ref, who, place = a_refs[at + 1], 1 - core, mirror
                    put(e, who, 0, ref[place * UA : place * UA + UA, :])

    put(0, core, UA, x0[...])
    put(0, 1 - core, UA, x0b[...])
    put(1, core, UA, xd[...])
    put(1, 1 - core, UA, xdb[...])
    put(2, 1 - core, UA, xs[...])
    put(2, core, UA, xsb[...])
    put(3, core, UA, xf[...])
    put(3, 1 - core, UA, xfb[...])
    tile = lax.dot_general(left[...], right[...], NT, preferred_element_type=F32)
    out[...] = (tile * (1.0 / 896.0)).astype(BF16)


def tile(where, rows, a_parts, b_parts, numbers, base, before=None):
    first = pl.BlockSpec((UB, 896), lambda s, w: (w[47 + base + s], 0))
    turned = pl.BlockSpec((UB, 896), lambda s, w: (w[35 + w[47 + base + s]], 0))
    operands = [*rows, *a_parts, *b_parts]
    specs = [whole(*part.shape) for part in rows + a_parts]
    specs += [first] * 4 + [turned, turned, first, turned]
    aliases = {}
    if before is not None:
        aliases = {1 + len(operands): 0}
        operands.append(before)
        specs.append(pl.BlockSpec(memory_space=pl.ANY))
    return pl.pallas_call(
        functools.partial(tile_kernel, numbers),
        out_shape=jax.ShapeDtypeStruct((448, 7168), BF16),
        grid_spec=pltpu.PrefetchScalarGridSpec(
            num_scalar_prefetch=1,
            grid=(len(numbers),),
            in_specs=specs,
            out_specs=pl.BlockSpec((448, 896), lambda s, w: (0, w[27 + w[47 + base + s]])),
            scratch_shapes=[pltpu.VMEM((448, 896), BF16), pltpu.VMEM((896, 896), BF16)],
        ),
        input_output_aliases=aliases,
        compiler_params=params(18),
        cost_estimate=cost(2 * len(numbers), len(numbers)),
        name="tile",
    )(where, *operands)


def body(activations, gate_weight, up_weight, anchor_states, token_ids, anchor_layer, token_weight):
    z, x = lax.axis_index("z"), lax.axis_index("x")
    core, y = lax.axis_index("core"), lax.axis_index("y")

    def around(me, size, offs):
        return [(me + off) % size for off in offs]

    xs, ys = around(x, NX, OFF4), around(y, NY, OFF4)
    left_y, left_core = z // 2, z % 2
    place = sum((ys[p] == left_y) * p for p in range(4))
    side = 1 - 2 * core
    x_pair = [x, (x - side) % NX, (x + side) % NX, (x + 2) % NX]
    z_pair = [(z - side * h) % NZ for h in range(4)] + [(z + side * h) % NZ for h in (1, 2, 3)] + [(z + 4) % NZ]
    table = [0] * 16 + [core, place, left_core] + x_pair + ys + z_pair
    table += list(TURN) + xs + list(EARLY + LATE)
    where = jnp.stack([jnp.asarray(v, jnp.int32) for v in table])

    others = swap_core(activations)
    pair = jnp.where(
        core == 0, jnp.concatenate([activations, others], 0), jnp.concatenate([others, activations], 0)
    )
    half = lax.dynamic_slice_in_dim(pair, core * 1024, 1024, 1)
    reach = [pair_step(pair, "z", hop) for hop in (1, 2, 3)]
    far = pair_step(half, "z", 4)
    *reach, far = lax.optimization_barrier((*reach, far))
    turned = swap_core(lax.dynamic_slice_in_dim(jnp.stack(reach), (1 - core) * 1024, 1024, 2))
    line = lineup(where, half, *reach, turned, far).reshape(224, 1024)

    gate_t, up_t = gate_weight.T, up_weight.T
    theirs = swap_core(away_half(where, gate_t, up_t))

    a_near = join([(block, 0, 224) for block in direct(line[:, :512], "x")]).reshape(4, 224, 512)
    b_near = join([(block, 0, 224) for block in direct(line[:, 512:], "y")]).reshape(4, 224, 512)
    a_near, b_near, theirs, token_ids, anchor_layer = lax.optimization_barrier(
        (a_near, b_near, theirs, token_ids, anchor_layer)
    )
    weights = pack_weights(where, gate_t, up_t, theirs)

    def reorder(ids):
        return ids.reshape(NZ, NX, 28).transpose(1, 0, 2).reshape(896)

    padded = jnp.pad(anchor_states, ((0, 0), (0, 16)))
    target = padded[reorder(anchor_layer)]
    scale = jnp.broadcast_to(token_weight[reorder(token_ids)][:, None], (896, 128))

    a_up, a_down = shift(a_near, "y", NY, 1), shift(a_near, "y", NY, -1)
    b_up, b_down = shift(b_near, "x", NX, 1), shift(b_near, "x", NX, -1)
    a_up, a_down, b_up, b_down, weights, target, scale = lax.optimization_barrier(
        (a_up, a_down, b_up, b_down, weights, target, scale)
    )
    a_parts = [a_near, a_up, a_down, shift(a_up[:2], "y", NY, 1), shift(a_down[2:], "y", NY, -1)]
    b_parts = [b_near, b_up, b_down, shift(b_up[:2], "x", NX, 1), shift(b_down[2:], "x", NX, -1)]
    own, sib = near_product(a_parts[:3], b_parts[:3], weights)
    own, sib = far_product(where, a_parts[3:], b_parts[3:], weights, own, sib)
    grads = gradient(own, swap_core(sib), target, scale)

    mates = swap_core(grads)
    x_near = pair_step(jnp.concatenate([grads[:UA], mates[:UA]], 0), "x", 1)
    x_far = pair_step(grads[:UA], "x", 2)
    x_turned, x_last = swap_core(x_near), swap_core(x_far)
    by_x = join(
        [(grads, 0, UA), (x_near, 0, UA), (x_turned, UA, UA), (x_far, 0, UA)]
        + [(mates, 0, UA), (x_near, UA, UA), (x_turned, 0, UA), (x_last, 0, UA)]
    )
    both = jnp.concatenate([grads[UA:], mates[UA:]], 0)
    z_near = [pair_step(both, "z", hop) for hop in (1, 2, 3)]
    z_far = pair_step(grads[UA:], "z", 4)
    z_turned, z_last = [swap_core(block) for block in z_near], swap_core(z_far)
    mine = join([(grads, UA, UB)] + [(b, 0, UB) for b in z_near] + [(b, UB, UB) for b in z_turned] + [(z_far, 0, UB)])
    others = join([(mates, UA, UB)] + [(b, UB, UB) for b in z_near] + [(b, 0, UB) for b in z_turned] + [(z_last, 0, UB)])

    hold = lax.optimization_barrier
    by_x, mine, others, grads, where_late = hold((by_x, mine, others, grads, where))
    z_one, x_one = pair_step(by_x, "z", 1), pair_step(mine, "x", 1)
    y_up, y_down = shift(grads, "y", NY, 1), shift(grads, "y", NY, -1)
    z_one, x_one, others, y_up, y_down, where_late = hold((z_one, x_one, others, y_up, y_down, where_late))

    z_two, x_more = pair_step(z_one, "z", 1), pair_step(others, "x", 1)
    z_one_b, x_one_b = swap_core(z_one), swap_core(x_one)
    y_low, y_high = shift(y_up[:48], "y", NY, 1), shift(y_down[48:], "y", NY, -1)
    chunks = pick(where_late, a_parts, b_parts)
    z_two, x_more, x_one, z_one_b, x_one_b, y_low, y_high, chunks = hold(
        (z_two, x_more, x_one, z_one_b, x_one_b, y_low, y_high, chunks)
    )
    z_three, x_two = pair_step(z_two, "z", 1), pair_step(x_one, "x", 1)
    z_two_b, x_more_b, chunks_b = swap_core(z_two), swap_core(x_more), swap_core(chunks)
    z_three, x_two, z_two_b, x_more_b, chunks_b = hold((z_three, x_two, z_two_b, x_more_b, chunks_b))

    z_four = pair_step(z_three[: 4 * UA], "z", 1)
    z_three_b, x_two_b = swap_core(z_three), swap_core(x_two)
    act_covariance = covariance(where, chunks, chunks_b)
    rows = [grads, y_up, y_down, y_low, y_high]
    x_all = [mine, others, x_one, x_more, x_one_b, x_more_b, x_two, x_two_b]
    columns = tile(where, rows, [by_x, z_one, z_two, z_one_b, z_two_b], x_all, EARLY, 0)
    late = [z_three, z_three_b, z_four, swap_core(z_four)]
    return act_covariance, tile(where, rows, late, x_all, LATE, len(EARLY), columns)


def solution(mesh):
    fine = Mesh(mesh.devices.reshape(NZ, NX, NC, NY), ("z", "x", "core", "y"))
    dp = ("z", "x", "core")
    units = P(None, dp + ("y",))
    in_specs = (P(dp, "y"), units, units, units, P(), P(), P())
    out_specs = (P(dp, "y"), P(dp, "y"))
    return jax.shard_map(body, mesh=fine, in_specs=in_specs, out_specs=out_specs, check_vma=False)
```

```python
import functools

import jax
import jax.numpy as jnp
from jax import lax
from jax.experimental import pallas as pl
from jax.experimental.pallas import tpu as pltpu
from jax.sharding import Mesh, PartitionSpec as P

NZ, NX, NC, NY = 8, 4, 2, 4
OFF4 = (0, 3, 1, 2)
F32, BF16 = jnp.float32, jnp.bfloat16


def shift(x, axis, size, step):
    return lax.ppermute(x, axis, [(i, (i + step) % size) for i in range(size)])


def swap_core(x):
    return lax.ppermute(x, "core", [(0, 1), (1, 0)])


def pair_step(x, axis, hop):
    size = {"x": NX, "z": NZ}[axis]
    perm = [(i * 2 + c, (i + s) % size * 2 + c) for c, s in ((0, hop), (1, -hop)) for i in range(size)]
    return lax.ppermute(x, (axis, "core"), perm)


def direct(x, axis):
    return [x] + [shift(x, axis, 4, step) for step in (1, -1, 2)]


def ring(x, axis, size, half):
    found = {0: x}
    left = right = x
    for hop in range(1, size // 2):
        left = shift(left, axis, size, 1)
        right = shift(right, axis, size, -1)
        found[size - hop] = left
        found[hop] = right
    found[size // 2] = (
        shift(left[:half], axis, size, 1),
        shift(right[half:], axis, size, -1),
    )
    return found


def flat(found, order):
    parts = []
    for off in order:
        block = found[off]
        parts += list(block) if isinstance(block, tuple) else [block]
    return parts


NT = (((1,), (1,)), ((), ()))
SCALARS = pl.BlockSpec(memory_space=pltpu.SMEM)


def params(mib):
    return pltpu.CompilerParams(vmem_limit_bytes=mib << 20)


def cost(mib, gflop=0):
    return pl.CostEstimate(flops=gflop << 30, bytes_accessed=mib << 20, transcendentals=0)


def whole(*shape):
    return pl.BlockSpec(shape, lambda *_: (0,) * len(shape))


def join_kernel(pieces, *refs):
    out = refs[-1]
    at = 0
    for number, first, count in pieces:
        out[at : at + count] = refs[number][first : first + count]
        at += count


def join(pieces):
    arrays, plan = [], []
    for array, first, count in pieces:
        number = next((i for i, seen in enumerate(arrays) if seen is array), len(arrays))
        if number == len(arrays):
            arrays.append(array)
        plan.append((number, first, count))
    rows = sum(count for _, _, count in plan)
    return pl.pallas_call(
        functools.partial(join_kernel, plan),
        out_shape=jax.ShapeDtypeStruct((rows,) + arrays[0].shape[1:], BF16),
        compiler_params=params(8),
        cost_estimate=cost(2),
        name="join",
    )(*arrays)


def lineup_kernel(where, mine, one, two, three, turned, far, out):
    lanes = pl.ds(pl.multiple_of(where[16] * 1024, 1024), 1024)
    out[where[27]] = mine[...]
    for number, ref in enumerate((one, two, three)):
        out[where[28 + number]] = ref[:, lanes]
        out[where[31 + number]] = turned[number]
    out[where[34]] = far[...]


def lineup(where, *blocks):
    return pl.pallas_call(
        lineup_kernel,
        out_shape=jax.ShapeDtypeStruct((8, 28, 1024), BF16),
        in_specs=[SCALARS] + [whole(*block.shape) for block in blocks],
        compiler_params=params(6),
        name="lineup",
    )(where, *blocks)


def away_kernel(where, gate, up, out):
    for part in range(4):
        lanes = pl.ds(pl.multiple_of(part * 2048 + (1 - where[16]) * 1024, 1024), 1024)
        out[part, 0:112, :] = gate[:, lanes]
        out[part, 112:224, :] = up[:, lanes]


def away_half(where, gate_t, up_t):
    return pl.pallas_call(
        away_kernel,
        out_shape=jax.ShapeDtypeStruct((4, 224, 1024), BF16),
        in_specs=[SCALARS, whole(*gate_t.shape), whole(*up_t.shape)],
        compiler_params=params(10),
        cost_estimate=cost(6),
        name="away_half",
    )(where, gate_t, up_t)


def pack_kernel(where, gate, up, sib, out):
    blank = jnp.zeros((16, 1024), BF16)
    for k in range(4):
        part = where[23 + k]
        lanes = pl.ds(pl.multiple_of(part * 2048 + where[16] * 1024, 1024), 1024)
        pieces = (gate[:, lanes], up[:, lanes], sib[part, 0:112, :], sib[part, 112:224, :])
        for number, piece in enumerate(pieces):
            out[k, number * 128 : number * 128 + 112, :] = piece
            out[k, number * 128 + 112 : number * 128 + 128, :] = blank


def pack_weights(where, gate_t, up_t, sib):
    return pl.pallas_call(
        pack_kernel,
        out_shape=jax.ShapeDtypeStruct((4, 512, 1024), BF16),
        in_specs=[SCALARS, whole(*gate_t.shape), whole(*up_t.shape), whole(*sib.shape)],
        compiler_params=params(14),
        cost_estimate=cost(12),
        name="pack_weights",
    )(where, gate_t, up_t, sib)


def near_kernel(a0, a1, a2, b0, b1, b2, w, own, sib):
    for p, ref in enumerate((a0, a1, a2)):
        block = ref[...].reshape(896, 512)
        part = lax.dot_general(block, w[p, :, 0:512], NT, preferred_element_type=F32)
        if p == 0:
            own[...] = part[:, :256]
            sib[...] = part[:, 256:]
        else:
            own[...] += part[:, :256]
            sib[...] += part[:, 256:]
    for e, ref in enumerate((b0, b1, b2)):
        rows = slice(e * 224, e * 224 + 224)
        for p in range(4):
            part = lax.dot_general(ref[p], w[p, :, 512:1024], NT, preferred_element_type=F32)
            own[rows, :] += part[:, :256]
            sib[rows, :] += part[:, 256:]


def near_product(a_parts, b_parts, w):
    out = jax.ShapeDtypeStruct((896, 256), F32)
    return pl.pallas_call(
        near_kernel,
        out_shape=(out, out),
        compiler_params=params(22),
        cost_estimate=cost(12, 3),
        name="near_product",
    )(*a_parts, *b_parts, w)


def far_kernel(where, a_low, a_high, b_low, b_high, w, own_in, sib_in, own, sib):
    for e in range(4):
        at = slice(e * 224, e * 224 + 224)
        rows = pl.ds(pl.multiple_of(where[43 + e] * 224, 16), 224)
        block = (a_low, a_high)[e // 2][e % 2]
        part = lax.dot_general(block, w[3, :, 0:512], NT, preferred_element_type=F32)
        if e == 3:
            for p in range(4):
                more = (b_low, b_high)[p // 2][p % 2]
                part += lax.dot_general(more, w[p, :, 512:1024], NT, preferred_element_type=F32)
        own[rows, :] = own_in[at, :] + part[:, :256]
        sib[rows, :] = sib_in[at, :] + part[:, 256:]


def far_product(where, a_parts, b_parts, w, own, sib):
    out = jax.ShapeDtypeStruct((896, 256), F32)
    operands = (*a_parts, *b_parts, w, own, sib)
    return pl.pallas_call(
        far_kernel,
        out_shape=(out, out),
        in_specs=[SCALARS] + [whole(*operand.shape) for operand in operands],
        compiler_params=params(18),
        cost_estimate=cost(8, 1),
        name="far_product",
    )(where, *operands)


def gradient_kernel(own, other, target, scale, out):
    both = own[...] + other[...]
    gate, up = both[:, :128], both[:, 128:]
    sig = jax.nn.sigmoid(gate)
    hidden = gate * sig * up
    loss_grad = scale[...] * (hidden - target[...].astype(F32))
    grad = loss_grad * up * sig * (1.0 + gate * (1.0 - sig))
    out[...] = jnp.transpose(grad)[:112, :].astype(BF16)


def gradient(own, other, target, scale):
    return pl.pallas_call(
        gradient_kernel,
        out_shape=jax.ShapeDtypeStruct((112, 896), BF16),
        compiler_params=params(10),
        name="gradient",
    )(own, other, target, scale)


def pick_kernel(where, *refs):
    a_refs, b_refs, out = refs[0:5], refs[5:10], refs[10]
    x = where[43]

    def rows(e):
        return pl.ds(pl.multiple_of(where[43 + e] * 224, 16), 224)

    for e in range(4):
        out[rows(e), 0:512] = a_refs[0][e]
        out[rows(e), 512:1024] = b_refs[e][0]
    lanes = pl.ds(pl.multiple_of(x % 2 * 256, 256), 256)
    for p in range(4):

        @pl.when((where[17] == p) & (x < 2))
        def _():
            for e in range(4):
                ref, row = (a_refs[p], e) if p < 3 else (a_refs[3 + e // 2], e % 2)
                out[rows(e), 1024:1280] = ref[row, :, lanes]

        @pl.when((where[17] == p) & (x >= 2))
        def _():
            for e in range(4):
                ref, row = (b_refs[e], p) if e < 3 else (b_refs[3 + p // 2], p % 2)
                out[rows(e), 1024:1280] = ref[row, :, lanes]


def pick(where, a_parts, b_parts):
    operands = (*a_parts, *b_parts)
    return pl.pallas_call(
        pick_kernel,
        out_shape=jax.ShapeDtypeStruct((896, 1280), BF16),
        in_specs=[SCALARS] + [whole(*operand.shape) for operand in operands],
        compiler_params=params(14),
        cost_estimate=cost(12),
        name="pick",
    )(where, *operands)


def covariance_kernel(where, mine, other, mine_left, other_left, out, left):
    step = pl.program_id(0)

    @pl.when(step == 0)
    def _():
        keep = where[18] == where[16]
        both = jnp.where(keep, mine_left[...], other_left[...]).astype(F32)
        side = jnp.where(where[16] == 0, both[:, :128], both[:, 128:])
        left[...] = jnp.transpose(side).astype(BF16)

    right = jnp.where(step % 2 == 0, mine[...], other[...])
    tile = lax.dot_general(
        left[...], right, (((1,), (0,)), ((), ())), preferred_element_type=F32
    )
    out[...] = tile * (1.0 / 896.0)


def covariance(where, mine, other):
    chunk = (896, 256)
    return pl.pallas_call(
        covariance_kernel,
        out_shape=jax.ShapeDtypeStruct((128, 2048), F32),
        grid_spec=pltpu.PrefetchScalarGridSpec(
            num_scalar_prefetch=1,
            grid=(8,),
            in_specs=[
                pl.BlockSpec(chunk, lambda s, w: (0, s // 2)),
                pl.BlockSpec(chunk, lambda s, w: (0, s // 2)),
                pl.BlockSpec(chunk, lambda s, w: (0, 4)),
                pl.BlockSpec(chunk, lambda s, w: (0, 4)),
            ],
            out_specs=pl.BlockSpec(
                (128, 256), lambda s, w: (0, s // 2 + 4 * ((w[16] + s % 2) % 2))
            ),
            scratch_shapes=[pltpu.VMEM((128, 896), BF16)],
        ),
        compiler_params=params(8),
        cost_estimate=cost(8, 1),
        name="covariance",
    )(where, mine, other, mine, other)


UA, UB = 64, 48
TURN = (0, 4, 5, 6, 1, 2, 3, 7)
EARLY, LATE = (0, 1, 2, 4, 5), (3, 6, 7)


def tile_kernel(numbers, where, *refs):
    rows, refs = refs[0:5], refs[5:]
    count = sum(2 if number == 7 else 1 for number in numbers)
    a_refs, refs = refs[0:count], refs[count:]
    (x0, x0b, xd, xdb, xs, xsb, xf, xfb) = refs[0:8]
    out, left, right = refs[-3:]
    step = pl.program_id(0)
    core = where[16]

    def put(slot_x, who, first, value):
        base = (where[19 + slot_x] * 2 + who) * 112 + first
        right[pl.ds(pl.multiple_of(base, 16), value.shape[0]), :] = value

    @pl.when(step == 0)
    def _():
        for number, ref in enumerate(rows):
            base = where[23 + min(number, 3)] * 112 + (48 if number == 4 else 0)
            left[pl.ds(pl.multiple_of(base, 16), ref.shape[0]), :] = ref[...]

    for at, number in enumerate(numbers):

        @pl.when(step == at)
        def _():
            for e in range(4):
                mirror = (0, 2, 1, 3)[e]
                for half in range(2):
                    ref = a_refs[at]
                    if number < 4:
                        who, place = (core, 1 - core)[half], half * 4 + e
                    elif number < 7:
                        who, place = (1 - core, core)[half], half * 4 + mirror
                    elif half == 0:
                        who, place = core, e
                    else:
                        ref, who, place = a_refs[at + 1], 1 - core, mirror
                    put(e, who, 0, ref[place * UA : place * UA + UA, :])

    put(0, core, UA, x0[...])
    put(0, 1 - core, UA, x0b[...])
    put(1, core, UA, xd[...])
    put(1, 1 - core, UA, xdb[...])
    put(2, 1 - core, UA, xs[...])
    put(2, core, UA, xsb[...])
    put(3, core, UA, xf[...])
    put(3, 1 - core, UA, xfb[...])
    tile = lax.dot_general(left[...], right[...], NT, preferred_element_type=F32)
    out[...] = (tile * (1.0 / 896.0)).astype(BF16)


def tile(where, rows, a_parts, b_parts, numbers, base, before=None):
    first = pl.BlockSpec((UB, 896), lambda s, w: (w[47 + base + s], 0))
    turned = pl.BlockSpec((UB, 896), lambda s, w: (w[35 + w[47 + base + s]], 0))
    operands = [*rows, *a_parts, *b_parts]
    specs = [whole(*part.shape) for part in rows + a_parts]
    specs += [first] * 4 + [turned, turned, first, turned]
    aliases = {}
    if before is not None:
        aliases = {1 + len(operands): 0}
        operands.append(before)
        specs.append(pl.BlockSpec(memory_space=pl.ANY))
    return pl.pallas_call(
        functools.partial(tile_kernel, numbers),
        out_shape=jax.ShapeDtypeStruct((448, 7168), BF16),
        grid_spec=pltpu.PrefetchScalarGridSpec(
            num_scalar_prefetch=1,
            grid=(len(numbers),),
            in_specs=specs,
            out_specs=pl.BlockSpec((448, 896), lambda s, w: (0, w[27 + w[47 + base + s]])),
            scratch_shapes=[pltpu.VMEM((448, 896), BF16), pltpu.VMEM((896, 896), BF16)],
        ),
        input_output_aliases=aliases,
        compiler_params=params(18),
        cost_estimate=cost(2 * len(numbers), len(numbers)),
        name="tile",
    )(where, *operands)


def body(activations, gate_weight, up_weight, anchor_states, token_ids, anchor_layer, token_weight):
    z, x = lax.axis_index("z"), lax.axis_index("x")
    core, y = lax.axis_index("core"), lax.axis_index("y")

    def around(me, size, offs):
        return [(me + off) % size for off in offs]

    xs, ys = around(x, NX, OFF4), around(y, NY, OFF4)
    left_y, left_core = z // 2, z % 2
    place = sum((ys[p] == left_y) * p for p in range(4))
    side = 1 - 2 * core
    x_pair = [x, (x - side) % NX, (x + side) % NX, (x + 2) % NX]
    z_pair = [(z - side * h) % NZ for h in range(4)] + [(z + side * h) % NZ for h in (1, 2, 3)] + [(z + 4) % NZ]
    table = [0] * 16 + [core, place, left_core] + x_pair + ys + z_pair
    table += list(TURN) + xs + list(EARLY + LATE)
    where = jnp.stack([jnp.asarray(v, jnp.int32) for v in table])

    others = swap_core(activations)
    pair = jnp.where(
        core == 0, jnp.concatenate([activations, others], 0), jnp.concatenate([others, activations], 0)
    )
    half = lax.dynamic_slice_in_dim(pair, core * 1024, 1024, 1)
    reach = [pair_step(pair, "z", hop) for hop in (1, 2, 3)]
    far = pair_step(half, "z", 4)
    *reach, far = lax.optimization_barrier((*reach, far))
    turned = swap_core(lax.dynamic_slice_in_dim(jnp.stack(reach), (1 - core) * 1024, 1024, 2))
    line = lineup(where, half, *reach, turned, far).reshape(224, 1024)

    gate_t, up_t = gate_weight.T, up_weight.T
    theirs = swap_core(away_half(where, gate_t, up_t))

    def gather(block, axis):
        parts = flat(ring(block, axis, 4, 112), OFF4)
        return join([(part, 0, part.shape[0]) for part in parts]).reshape(4, 224, 512)

    a_near, b_near = gather(line[:, :512], "x"), gather(line[:, 512:], "y")
    a_near, b_near, theirs, token_ids, anchor_layer = lax.optimization_barrier(
        (a_near, b_near, theirs, token_ids, anchor_layer)
    )
    weights = pack_weights(where, gate_t, up_t, theirs)

    def reorder(ids):
        return ids.reshape(NZ, NX, 28).transpose(1, 0, 2).reshape(896)

    padded = jnp.pad(anchor_states, ((0, 0), (0, 16)))
    target = padded[reorder(anchor_layer)]
    scale = jnp.broadcast_to(token_weight[reorder(token_ids)][:, None], (896, 128))

    a_up, a_down = shift(a_near, "y", NY, 1), shift(a_near, "y", NY, -1)
    b_up, b_down = shift(b_near, "x", NX, 1), shift(b_near, "x", NX, -1)
    b_up, b_down, weights, target, scale = lax.optimization_barrier(
        (b_up, b_down, weights, target, scale)
    )
    a_parts = [a_near, a_up, a_down, shift(a_up[:2], "y", NY, 1), shift(a_down[2:], "y", NY, -1)]
    b_parts = [b_near, b_up, b_down, shift(b_up[:2], "x", NX, 1), shift(b_down[2:], "x", NX, -1)]
    own, sib = near_product(a_parts[:3], b_parts[:3], weights)
    own, sib = far_product(where, a_parts[3:], b_parts[3:], weights, own, sib)
    grads = gradient(own, swap_core(sib), target, scale)

    mates = swap_core(grads)
    mates, where_late = lax.optimization_barrier((mates, where))
    chunks = pick(where_late, a_parts, b_parts)
    x_near = pair_step(jnp.concatenate([grads[:UA], mates[:UA]], 0), "x", 1)
    x_far = pair_step(grads[:UA], "x", 2)
    x_turned, x_last = swap_core(x_near), swap_core(x_far)
    by_x = join(
        [(grads, 0, UA), (x_near, 0, UA), (x_turned, UA, UA), (x_far, 0, UA)]
        + [(mates, 0, UA), (x_near, UA, UA), (x_turned, 0, UA), (x_last, 0, UA)]
    )
    both = jnp.concatenate([grads[UA:], mates[UA:]], 0)
    z_near = [pair_step(both, "z", hop) for hop in (1, 2, 3)]
    z_far = pair_step(grads[UA:], "z", 4)
    z_turned, z_last = [swap_core(block) for block in z_near], swap_core(z_far)
    mine = join([(grads, UA, UB)] + [(b, 0, UB) for b in z_near] + [(b, UB, UB) for b in z_turned] + [(z_far, 0, UB)])
    others = join([(mates, UA, UB)] + [(b, UB, UB) for b in z_near] + [(b, 0, UB) for b in z_turned] + [(z_last, 0, UB)])

    hold = lax.optimization_barrier
    by_x, mine, others, grads, chunks = hold((by_x, mine, others, grads, chunks))
    z_one, x_one, chunks_b = pair_step(by_x, "z", 1), pair_step(mine, "x", 1), swap_core(chunks)
    y_up, y_down = shift(grads, "y", NY, 1), shift(grads, "y", NY, -1)
    z_one, x_one, others, y_up, y_down, chunks_b = hold((z_one, x_one, others, y_up, y_down, chunks_b))

    z_two, x_more = pair_step(z_one, "z", 1), pair_step(others, "x", 1)
    z_one_b, x_one_b = swap_core(z_one), swap_core(x_one)
    y_high = shift(y_down[48:], "y", NY, -1)
    act_covariance = covariance(where, chunks, chunks_b)
    z_two, x_more, x_one, z_one_b, x_one_b, y_up, y_high, act_covariance = hold(
        (z_two, x_more, x_one, z_one_b, x_one_b, y_up, y_high, act_covariance)
    )
    z_three, x_two = pair_step(z_two, "z", 1), pair_step(x_one, "x", 1)
    z_two_b, x_more_b = swap_core(z_two), swap_core(x_more)
    y_low = shift(y_up[:48], "y", NY, 1)
    z_three, x_two, z_two_b, x_more_b, y_low = hold((z_three, x_two, z_two_b, x_more_b, y_low))

    z_four = pair_step(z_three[: 4 * UA], "z", 1)
    z_three_b, x_two_b = swap_core(z_three), swap_core(x_two)
    rows = [grads, y_up, y_down, y_low, y_high]
    x_all = [mine, others, x_one, x_more, x_one_b, x_more_b, x_two, x_two_b]
    columns = tile(where, rows, [by_x, z_one, z_two, z_one_b, z_two_b], x_all, EARLY, 0)
    z_four, columns = hold((z_four, columns))
    late = [z_three, z_three_b, z_four, swap_core(z_four)]
    return act_covariance, tile(where, rows, late, x_all, LATE, len(EARLY), columns)


def solution(mesh):
    fine = Mesh(mesh.devices.reshape(NZ, NX, NC, NY), ("z", "x", "core", "y"))
    dp = ("z", "x", "core")
    units = P(None, dp + ("y",))
    in_specs = (P(dp, "y"), units, units, units, P(), P(), P())
    out_specs = (P(dp, "y"), P(dp, "y"))
    return jax.shard_map(body, mesh=fine, in_specs=in_specs, out_specs=out_specs, check_vma=False)
```

```python
import functools

import jax
import jax.numpy as jnp
from jax import lax
from jax.experimental import pallas as pl
from jax.experimental.pallas import tpu as pltpu
from jax.sharding import Mesh, PartitionSpec as P

NZ, NX, NC, NY = 8, 4, 2, 4
OFF4 = (0, 3, 1, 2)
F32, BF16 = jnp.float32, jnp.bfloat16


def shift(x, axis, size, step):
    return lax.ppermute(x, axis, [(i, (i + step) % size) for i in range(size)])


def swap_core(x):
    return lax.ppermute(x, "core", [(0, 1), (1, 0)])


def pair_step(x, axis, hop):
    size = {"x": NX, "z": NZ}[axis]
    perm = [(i * 2 + c, (i + s) % size * 2 + c) for c, s in ((0, hop), (1, -hop)) for i in range(size)]
    return lax.ppermute(x, (axis, "core"), perm)


def direct(x, axis):
    return [x] + [shift(x, axis, 4, step) for step in (1, -1, 2)]


def ring(x, axis, size, half):
    found = {0: x}
    left = right = x
    for hop in range(1, size // 2):
        left = shift(left, axis, size, 1)
        right = shift(right, axis, size, -1)
        found[size - hop] = left
        found[hop] = right
    found[size // 2] = (
        shift(left[:half], axis, size, 1),
        shift(right[half:], axis, size, -1),
    )
    return found


def flat(found, order):
    parts = []
    for off in order:
        block = found[off]
        parts += list(block) if isinstance(block, tuple) else [block]
    return parts


NT = (((1,), (1,)), ((), ()))
SCALARS = pl.BlockSpec(memory_space=pltpu.SMEM)


def params(mib):
    return pltpu.CompilerParams(vmem_limit_bytes=mib << 20)


def cost(mib, gflop=0):
    return pl.CostEstimate(flops=gflop << 30, bytes_accessed=mib << 20, transcendentals=0)


def whole(*shape):
    return pl.BlockSpec(shape, lambda *_: (0,) * len(shape))


def join_kernel(pieces, *refs):
    out = refs[-1]
    at = 0
    for number, first, count in pieces:
        out[at : at + count] = refs[number][first : first + count]
        at += count


def join(pieces):
    arrays, plan = [], []
    for array, first, count in pieces:
        number = next((i for i, seen in enumerate(arrays) if seen is array), len(arrays))
        if number == len(arrays):
            arrays.append(array)
        plan.append((number, first, count))
    rows = sum(count for _, _, count in plan)
    return pl.pallas_call(
        functools.partial(join_kernel, plan),
        out_shape=jax.ShapeDtypeStruct((rows,) + arrays[0].shape[1:], BF16),
        compiler_params=params(8),
        cost_estimate=cost(2),
        name="join",
    )(*arrays)


def lineup_kernel(where, mine, one, two, three, turned, far, out):
    lanes = pl.ds(pl.multiple_of(where[16] * 1024, 1024), 1024)
    out[where[27]] = mine[...]
    for number, ref in enumerate((one, two, three)):
        out[where[28 + number]] = ref[:, lanes]
        out[where[31 + number]] = turned[number]
    out[where[34]] = far[...]


def lineup(where, *blocks):
    return pl.pallas_call(
        lineup_kernel,
        out_shape=jax.ShapeDtypeStruct((8, 28, 1024), BF16),
        in_specs=[SCALARS] + [whole(*block.shape) for block in blocks],
        compiler_params=params(6),
        name="lineup",
    )(where, *blocks)


def away_kernel(where, gate, up, out, sems):
    copies = []
    for part in range(4):
        lanes = pl.ds(pl.multiple_of(part * 2048 + (1 - where[16]) * 1024, 1024), 1024)
        for number, ref in enumerate((gate, up)):
            to = out.at[part, number * 112 : number * 112 + 112, :]
            copies.append(pltpu.make_async_copy(ref.at[:, lanes], to, sems.at[part * 2 + number]))
    for copy in copies:
        copy.start()
    for copy in copies:
        copy.wait()


def away_half(where, gate_t, up_t):
    anywhere = pl.BlockSpec(memory_space=pl.ANY)
    return pl.pallas_call(
        away_kernel,
        out_shape=jax.ShapeDtypeStruct((4, 224, 1024), BF16),
        in_specs=[SCALARS, anywhere, anywhere],
        scratch_shapes=[pltpu.SemaphoreType.DMA((8,))],
        compiler_params=params(56),
        cost_estimate=cost(4),
        name="away_half",
    )(where, gate_t, up_t)


def pack_kernel(where, gate, up, sib, out):
    blank = jnp.zeros((16, 1024), BF16)
    for k in range(4):
        part = where[23 + k]
        lanes = pl.ds(pl.multiple_of(part * 2048 + where[16] * 1024, 1024), 1024)
        pieces = (gate[:, lanes], up[:, lanes], sib[part, 0:112, :], sib[part, 112:224, :])
        for number, piece in enumerate(pieces):
            out[k, number * 128 : number * 128 + 112, :] = piece
            out[k, number * 128 + 112 : number * 128 + 128, :] = blank


def pack_weights(where, gate_t, up_t, sib):
    return pl.pallas_call(
        pack_kernel,
        out_shape=jax.ShapeDtypeStruct((4, 512, 1024), BF16),
        in_specs=[SCALARS, whole(*gate_t.shape), whole(*up_t.shape), whole(*sib.shape)],
        compiler_params=params(14),
        cost_estimate=cost(12),
        name="pack_weights",
    )(where, gate_t, up_t, sib)


def near_kernel(a0, a1, a2, b0, b1, b2, w, own, sib):
    for p, ref in enumerate((a0, a1, a2)):
        block = ref[...].reshape(896, 512)
        part = lax.dot_general(block, w[p, :, 0:512], NT, preferred_element_type=F32)
        if p == 0:
            own[...] = part[:, :256]
            sib[...] = part[:, 256:]
        else:
            own[...] += part[:, :256]
            sib[...] += part[:, 256:]
    for e, ref in enumerate((b0, b1, b2)):
        rows = slice(e * 224, e * 224 + 224)
        for p in range(4):
            part = lax.dot_general(ref[p], w[p, :, 512:1024], NT, preferred_element_type=F32)
            own[rows, :] += part[:, :256]
            sib[rows, :] += part[:, 256:]


def near_product(a_parts, b_parts, w):
    out = jax.ShapeDtypeStruct((896, 256), F32)
    return pl.pallas_call(
        near_kernel,
        out_shape=(out, out),
        compiler_params=params(22),
        cost_estimate=cost(12, 3),
        name="near_product",
    )(*a_parts, *b_parts, w)


def far_kernel(where, a_low, a_high, b_low, b_high, w, own_in, sib_in, own, sib):
    for e in range(4):
        at = slice(e * 224, e * 224 + 224)
        rows = pl.ds(pl.multiple_of(where[43 + e] * 224, 16), 224)
        block = (a_low, a_high)[e // 2][e % 2]
        part = lax.dot_general(block, w[3, :, 0:512], NT, preferred_element_type=F32)
        if e == 3:
            for p in range(4):
                more = (b_low, b_high)[p // 2][p % 2]
                part += lax.dot_general(more, w[p, :, 512:1024], NT, preferred_element_type=F32)
        own[rows, :] = own_in[at, :] + part[:, :256]
        sib[rows, :] = sib_in[at, :] + part[:, 256:]


def far_product(where, a_parts, b_parts, w, own, sib):
    out = jax.ShapeDtypeStruct((896, 256), F32)
    operands = (*a_parts, *b_parts, w, own, sib)
    return pl.pallas_call(
        far_kernel,
        out_shape=(out, out),
        in_specs=[SCALARS] + [whole(*operand.shape) for operand in operands],
        compiler_params=params(18),
        cost_estimate=cost(8, 1),
        name="far_product",
    )(where, *operands)


def gradient_kernel(own, other, target, scale, out):
    both = own[...] + other[...]
    gate, up = both[:, :128], both[:, 128:]
    sig = jax.nn.sigmoid(gate)
    hidden = gate * sig * up
    loss_grad = scale[...] * (hidden - target[...].astype(F32))
    grad = loss_grad * up * sig * (1.0 + gate * (1.0 - sig))
    out[...] = jnp.transpose(grad)[:112, :].astype(BF16)


def gradient(own, other, target, scale):
    return pl.pallas_call(
        gradient_kernel,
        out_shape=jax.ShapeDtypeStruct((112, 896), BF16),
        compiler_params=params(10),
        name="gradient",
    )(own, other, target, scale)


def pick_kernel(where, *refs):
    a_refs, b_refs, out = refs[0:5], refs[5:10], refs[10]
    x = where[43]

    def rows(e):
        return pl.ds(pl.multiple_of(where[43 + e] * 224, 16), 224)

    for e in range(4):
        out[rows(e), 0:512] = a_refs[0][e]
        out[rows(e), 512:1024] = b_refs[e][0]
    lanes = pl.ds(pl.multiple_of(x % 2 * 256, 256), 256)
    for p in range(4):

        @pl.when((where[17] == p) & (x < 2))
        def _():
            for e in range(4):
                ref, row = (a_refs[p], e) if p < 3 else (a_refs[3 + e // 2], e % 2)
                out[rows(e), 1024:1280] = ref[row, :, lanes]

        @pl.when((where[17] == p) & (x >= 2))
        def _():
            for e in range(4):
                ref, row = (b_refs[e], p) if e < 3 else (b_refs[3 + p // 2], p % 2)
                out[rows(e), 1024:1280] = ref[row, :, lanes]


def pick(where, a_parts, b_parts):
    operands = (*a_parts, *b_parts)
    return pl.pallas_call(
        pick_kernel,
        out_shape=jax.ShapeDtypeStruct((896, 1280), BF16),
        in_specs=[SCALARS] + [whole(*operand.shape) for operand in operands],
        compiler_params=params(14),
        cost_estimate=cost(12),
        name="pick",
    )(where, *operands)


def covariance_kernel(where, mine, other, mine_left, other_left, out, left):
    step = pl.program_id(0)

    @pl.when(step == 0)
    def _():
        keep = where[18] == where[16]
        both = jnp.where(keep, mine_left[...], other_left[...]).astype(F32)
        side = jnp.where(where[16] == 0, both[:, :128], both[:, 128:])
        left[...] = jnp.transpose(side).astype(BF16)

    right = jnp.where(step % 2 == 0, mine[...], other[...])
    tile = lax.dot_general(
        left[...], right, (((1,), (0,)), ((), ())), preferred_element_type=F32
    )
    out[...] = tile * (1.0 / 896.0)


def covariance(where, mine, other):
    chunk = (896, 256)
    return pl.pallas_call(
        covariance_kernel,
        out_shape=jax.ShapeDtypeStruct((128, 2048), F32),
        grid_spec=pltpu.PrefetchScalarGridSpec(
            num_scalar_prefetch=1,
            grid=(8,),
            in_specs=[
                pl.BlockSpec(chunk, lambda s, w: (0, s // 2)),
                pl.BlockSpec(chunk, lambda s, w: (0, s // 2)),
                pl.BlockSpec(chunk, lambda s, w: (0, 4)),
                pl.BlockSpec(chunk, lambda s, w: (0, 4)),
            ],
            out_specs=pl.BlockSpec(
                (128, 256), lambda s, w: (0, s // 2 + 4 * ((w[16] + s % 2) % 2))
            ),
            scratch_shapes=[pltpu.VMEM((128, 896), BF16)],
        ),
        compiler_params=params(8),
        cost_estimate=cost(8, 1),
        name="covariance",
    )(where, mine, other, mine, other)


UA, UB = 64, 48
TURN = (0, 4, 5, 6, 1, 2, 3, 7)
EARLY, LATE = (0, 1, 2, 4, 5), (3, 6, 7)


def tile_kernel(numbers, where, *refs):
    rows, refs = refs[0:5], refs[5:]
    count = sum(2 if number == 7 else 1 for number in numbers)
    a_refs, refs = refs[0:count], refs[count:]
    (x0, x0b, xd, xdb, xs, xsb, xf, xfb) = refs[0:8]
    out, left, right = refs[-3:]
    step = pl.program_id(0)
    core = where[16]

    def put(slot_x, who, first, value):
        base = (where[19 + slot_x] * 2 + who) * 112 + first
        right[pl.ds(pl.multiple_of(base, 16), value.shape[0]), :] = value

    @pl.when(step == 0)
    def _():
        for number, ref in enumerate(rows):
            base = where[23 + min(number, 3)] * 112 + (48 if number == 4 else 0)
            left[pl.ds(pl.multiple_of(base, 16), ref.shape[0]), :] = ref[...]

    for at, number in enumerate(numbers):

        @pl.when(step == at)
        def _():
            for e in range(4):
                mirror = (0, 2, 1, 3)[e]
                for half in range(2):
                    ref = a_refs[at]
                    if number < 4:
                        who, place = (core, 1 - core)[half], half * 4 + e
                    elif number < 7:
                        who, place = (1 - core, core)[half], half * 4 + mirror
                    elif half == 0:
                        who, place = core, e
                    else:
                        ref, who, place = a_refs[at + 1], 1 - core, mirror
                    put(e, who, 0, ref[place * UA : place * UA + UA, :])

    put(0, core, UA, x0[...])
    put(0, 1 - core, UA, x0b[...])
    put(1, core, UA, xd[...])
    put(1, 1 - core, UA, xdb[...])
    put(2, 1 - core, UA, xs[...])
    put(2, core, UA, xsb[...])
    put(3, core, UA, xf[...])
    put(3, 1 - core, UA, xfb[...])
    tile = lax.dot_general(left[...], right[...], NT, preferred_element_type=F32)
    out[...] = (tile * (1.0 / 896.0)).astype(BF16)


def tile(where, rows, a_parts, b_parts, numbers, base, before=None):
    first = pl.BlockSpec((UB, 896), lambda s, w: (w[47 + base + s], 0))
    turned = pl.BlockSpec((UB, 896), lambda s, w: (w[35 + w[47 + base + s]], 0))
    operands = [*rows, *a_parts, *b_parts]
    specs = [whole(*part.shape) for part in rows + a_parts]
    specs += [first] * 4 + [turned, turned, first, turned]
    aliases = {}
    if before is not None:
        aliases = {1 + len(operands): 0}
        operands.append(before)
        specs.append(pl.BlockSpec(memory_space=pl.ANY))
    return pl.pallas_call(
        functools.partial(tile_kernel, numbers),
        out_shape=jax.ShapeDtypeStruct((448, 7168), BF16),
        grid_spec=pltpu.PrefetchScalarGridSpec(
            num_scalar_prefetch=1,
            grid=(len(numbers),),
            in_specs=specs,
            out_specs=pl.BlockSpec((448, 896), lambda s, w: (0, w[27 + w[47 + base + s]])),
            scratch_shapes=[pltpu.VMEM((448, 896), BF16), pltpu.VMEM((896, 896), BF16)],
        ),
        input_output_aliases=aliases,
        compiler_params=params(18),
        cost_estimate=cost(2 * len(numbers), len(numbers)),
        name="tile",
    )(where, *operands)


def body(activations, gate_weight, up_weight, anchor_states, token_ids, anchor_layer, token_weight):
    z, x = lax.axis_index("z"), lax.axis_index("x")
    core, y = lax.axis_index("core"), lax.axis_index("y")

    def around(me, size, offs):
        return [(me + off) % size for off in offs]

    xs, ys = around(x, NX, OFF4), around(y, NY, OFF4)
    left_y, left_core = z // 2, z % 2
    place = sum((ys[p] == left_y) * p for p in range(4))
    side = 1 - 2 * core
    x_pair = [x, (x - side) % NX, (x + side) % NX, (x + 2) % NX]
    z_pair = [(z - side * h) % NZ for h in range(4)] + [(z + side * h) % NZ for h in (1, 2, 3)] + [(z + 4) % NZ]
    table = [0] * 16 + [core, place, left_core] + x_pair + ys + z_pair
    table += list(TURN) + xs + list(EARLY + LATE)
    where = jnp.stack([jnp.asarray(v, jnp.int32) for v in table])

    others = swap_core(activations)
    pair = jnp.where(
        core == 0, jnp.concatenate([activations, others], 0), jnp.concatenate([others, activations], 0)
    )
    half = lax.dynamic_slice_in_dim(pair, core * 1024, 1024, 1)
    reach = [pair_step(pair, "z", hop) for hop in (1, 2, 3)]
    far = pair_step(half, "z", 4)
    *reach, far = lax.optimization_barrier((*reach, far))
    turned = swap_core(lax.dynamic_slice_in_dim(jnp.stack(reach), (1 - core) * 1024, 1024, 2))
    line = lineup(where, half, *reach, turned, far).reshape(224, 1024)

    gate_t, up_t = gate_weight.T, up_weight.T
    theirs = swap_core(away_half(where, gate_t, up_t))

    def gather(block, axis):
        parts = flat(ring(block, axis, 4, 112), OFF4)
        return join([(part, 0, part.shape[0]) for part in parts]).reshape(4, 224, 512)

    a_near, b_near = gather(line[:, :512], "x"), gather(line[:, 512:], "y")
    a_near, b_near, theirs, token_ids, anchor_layer = lax.optimization_barrier(
        (a_near, b_near, theirs, token_ids, anchor_layer)
    )
    weights = pack_weights(where, gate_t, up_t, theirs)

    def reorder(ids):
        return ids.reshape(NZ, NX, 28).transpose(1, 0, 2).reshape(896)

    padded = jnp.pad(anchor_states, ((0, 0), (0, 16)))
    target = padded[reorder(anchor_layer)]
    scale = jnp.broadcast_to(token_weight[reorder(token_ids)][:, None], (896, 128))

    a_up, a_down = shift(a_near, "y", NY, 1), shift(a_near, "y", NY, -1)
    b_up, b_down = shift(b_near, "x", NX, 1), shift(b_near, "x", NX, -1)
    b_up, b_down, weights, target, scale = lax.optimization_barrier(
        (b_up, b_down, weights, target, scale)
    )
    a_parts = [a_near, a_up, a_down, shift(a_up[:2], "y", NY, 1), shift(a_down[2:], "y", NY, -1)]
    b_parts = [b_near, b_up, b_down, shift(b_up[:2], "x", NX, 1), shift(b_down[2:], "x", NX, -1)]
    own, sib = near_product(a_parts[:3], b_parts[:3], weights)
    own, sib = far_product(where, a_parts[3:], b_parts[3:], weights, own, sib)
    grads = gradient(own, swap_core(sib), target, scale)

    mates = swap_core(grads)
    mates, grads, where_late = lax.optimization_barrier((mates, grads, where))
    x_far, z_far = pair_step(grads[:UA], "x", 2), pair_step(grads[UA:], "z", 4)
    chunks = pick(where_late, a_parts, b_parts)
    x_near = pair_step(jnp.concatenate([grads[:UA], mates[:UA]], 0), "x", 1)
    x_turned, x_last = swap_core(x_near), swap_core(x_far)
    by_x = join(
        [(grads, 0, UA), (x_near, 0, UA), (x_turned, UA, UA), (x_far, 0, UA)]
        + [(mates, 0, UA), (x_near, UA, UA), (x_turned, 0, UA), (x_last, 0, UA)]
    )
    both = jnp.concatenate([grads[UA:], mates[UA:]], 0)
    z_near = [pair_step(both, "z", hop) for hop in (1, 2)]
    x_far, both_late, chunks = lax.optimization_barrier((x_far, both, chunks))
    z_near.append(pair_step(both_late, "z", 3))
    z_turned, z_last = [swap_core(block) for block in z_near], swap_core(z_far)
    mine = join([(grads, UA, UB)] + [(b, 0, UB) for b in z_near] + [(b, UB, UB) for b in z_turned] + [(z_far, 0, UB)])
    others = join([(mates, UA, UB)] + [(b, UB, UB) for b in z_near] + [(b, 0, UB) for b in z_turned] + [(z_last, 0, UB)])

    hold = lax.optimization_barrier
    by_x, mine, others, grads, chunks = hold((by_x, mine, others, grads, chunks))
    z_one, x_one, chunks_b = pair_step(by_x, "z", 1), pair_step(mine, "x", 1), swap_core(chunks)
    y_up, y_down = shift(grads, "y", NY, 1), shift(grads, "y", NY, -1)
    z_one, x_one, others, y_up, y_down, chunks_b = hold((z_one, x_one, others, y_up, y_down, chunks_b))

    z_two, x_more = pair_step(z_one, "z", 1), pair_step(others, "x", 1)
    z_one_b, x_one_b = swap_core(z_one), swap_core(x_one)
    y_high = shift(y_down[48:], "y", NY, -1)
    act_covariance = covariance(where, chunks, chunks_b)
    z_two, x_more, x_one, z_one_b, x_one_b, y_up, y_high, act_covariance = hold(
        (z_two, x_more, x_one, z_one_b, x_one_b, y_up, y_high, act_covariance)
    )
    z_three, x_two = pair_step(z_two, "z", 1), pair_step(x_one, "x", 1)
    z_two_b, x_more_b = swap_core(z_two), swap_core(x_more)
    y_low = shift(y_up[:48], "y", NY, 1)
    z_three, x_two, z_two_b, x_more_b, y_low = hold((z_three, x_two, z_two_b, x_more_b, y_low))

    z_four = pair_step(z_three[: 4 * UA], "z", 1)
    z_three_b, x_two_b = swap_core(z_three), swap_core(x_two)
    rows = [grads, y_up, y_down, y_low, y_high]
    x_all = [mine, others, x_one, x_more, x_one_b, x_more_b, x_two, x_two_b]
    columns = tile(where, rows, [by_x, z_one, z_two, z_one_b, z_two_b], x_all, EARLY, 0)
    z_four, columns = hold((z_four, columns))
    late = [z_three, z_three_b, z_four, swap_core(z_four)]
    return act_covariance, tile(where, rows, late, x_all, LATE, len(EARLY), columns)


def solution(mesh):
    fine = Mesh(mesh.devices.reshape(NZ, NX, NC, NY), ("z", "x", "core", "y"))
    dp = ("z", "x", "core")
    units = P(None, dp + ("y",))
    in_specs = (P(dp, "y"), units, units, units, P(), P(), P())
    out_specs = (P(dp, "y"), P(dp, "y"))
    return jax.shard_map(body, mesh=fine, in_specs=in_specs, out_specs=out_specs, check_vma=False)
```

```python
import functools

import jax
import jax.numpy as jnp
from jax import lax
from jax.experimental import pallas as pl
from jax.experimental.pallas import tpu as pltpu
from jax.sharding import Mesh, PartitionSpec as P

NZ, NX, NC, NY = 8, 4, 2, 4
OFF4 = (0, 3, 1, 2)
F32, BF16 = jnp.float32, jnp.bfloat16


def shift(x, axis, size, step):
    return lax.ppermute(x, axis, [(i, (i + step) % size) for i in range(size)])


def swap_core(x):
    return lax.ppermute(x, "core", [(0, 1), (1, 0)])


def pair_step(x, axis, hop):
    size = {"x": NX, "z": NZ}[axis]
    perm = [(i * 2 + c, (i + s) % size * 2 + c) for c, s in ((0, hop), (1, -hop)) for i in range(size)]
    return lax.ppermute(x, (axis, "core"), perm)


def direct(x, axis):
    return [x] + [shift(x, axis, 4, step) for step in (1, -1, 2)]


def ring(x, axis, size, half):
    found = {0: x}
    left = right = x
    for hop in range(1, size // 2):
        left = shift(left, axis, size, 1)
        right = shift(right, axis, size, -1)
        found[size - hop] = left
        found[hop] = right
    found[size // 2] = (
        shift(left[:half], axis, size, 1),
        shift(right[half:], axis, size, -1),
    )
    return found


def flat(found, order):
    parts = []
    for off in order:
        block = found[off]
        parts += list(block) if isinstance(block, tuple) else [block]
    return parts


NT = (((1,), (1,)), ((), ()))
SCALARS = pl.BlockSpec(memory_space=pltpu.SMEM)


def params(mib):
    return pltpu.CompilerParams(vmem_limit_bytes=mib << 20)


def cost(mib, gflop=0):
    return pl.CostEstimate(flops=gflop << 30, bytes_accessed=mib << 20, transcendentals=0)


def whole(*shape):
    return pl.BlockSpec(shape, lambda *_: (0,) * len(shape))


def join_kernel(pieces, *refs):
    out = refs[-1]
    at = 0
    for number, first, count in pieces:
        out[at : at + count] = refs[number][first : first + count]
        at += count


def join(pieces):
    arrays, plan = [], []
    for array, first, count in pieces:
        number = next((i for i, seen in enumerate(arrays) if seen is array), len(arrays))
        if number == len(arrays):
            arrays.append(array)
        plan.append((number, first, count))
    rows = sum(count for _, _, count in plan)
    return pl.pallas_call(
        functools.partial(join_kernel, plan),
        out_shape=jax.ShapeDtypeStruct((rows,) + arrays[0].shape[1:], BF16),
        compiler_params=params(8),
        cost_estimate=cost(2),
        name="join",
    )(*arrays)


def lineup_kernel(where, mine, one, two, three, turned, far, out):
    lanes = pl.ds(pl.multiple_of(where[16] * 1024, 1024), 1024)
    out[where[27]] = mine[...]
    for number, ref in enumerate((one, two, three)):
        out[where[28 + number]] = ref[:, lanes]
        out[where[31 + number]] = turned[number]
    out[where[34]] = far[...]


def lineup(where, *blocks):
    return pl.pallas_call(
        lineup_kernel,
        out_shape=jax.ShapeDtypeStruct((8, 28, 1024), BF16),
        in_specs=[SCALARS] + [whole(*block.shape) for block in blocks],
        compiler_params=params(6),
        name="lineup",
    )(where, *blocks)


def away_kernel(where, gate, up, out, sems):
    copies = []
    for part in range(4):
        lanes = pl.ds(pl.multiple_of(part * 2048 + (1 - where[16]) * 1024, 1024), 1024)
        for number, ref in enumerate((gate, up)):
            to = out.at[part, number * 112 : number * 112 + 112, :]
            copies.append(pltpu.make_async_copy(ref.at[:, lanes], to, sems.at[part * 2 + number]))
    for copy in copies:
        copy.start()
    for copy in copies:
        copy.wait()


def away_half(where, gate_t, up_t):
    anywhere = pl.BlockSpec(memory_space=pl.ANY)
    return pl.pallas_call(
        away_kernel,
        out_shape=jax.ShapeDtypeStruct((4, 224, 1024), BF16),
        in_specs=[SCALARS, anywhere, anywhere],
        scratch_shapes=[pltpu.SemaphoreType.DMA((8,))],
        compiler_params=params(56),
        cost_estimate=cost(4),
        name="away_half",
    )(where, gate_t, up_t)


def pack_kernel(where, gate, up, sib, out):
    blank = jnp.zeros((16, 1024), BF16)
    for k in range(4):
        part = where[23 + k]
        lanes = pl.ds(pl.multiple_of(part * 2048 + where[16] * 1024, 1024), 1024)
        pieces = (gate[:, lanes], up[:, lanes], sib[part, 0:112, :], sib[part, 112:224, :])
        for number, piece in enumerate(pieces):
            out[k, number * 128 : number * 128 + 112, :] = piece
            out[k, number * 128 + 112 : number * 128 + 128, :] = blank


def pack_weights(where, gate_t, up_t, sib):
    return pl.pallas_call(
        pack_kernel,
        out_shape=jax.ShapeDtypeStruct((4, 512, 1024), BF16),
        in_specs=[SCALARS, whole(*gate_t.shape), whole(*up_t.shape), whole(*sib.shape)],
        compiler_params=params(14),
        cost_estimate=cost(12),
        name="pack_weights",
    )(where, gate_t, up_t, sib)


def near_kernel(a0, a1, a2, b0, b1, b2, w, own, sib):
    for p, ref in enumerate((a0, a1, a2)):
        block = ref[...].reshape(896, 512)
        part = lax.dot_general(block, w[p, :, 0:512], NT, preferred_element_type=F32)
        if p == 0:
            own[...] = part[:, :256]
            sib[...] = part[:, 256:]
        else:
            own[...] += part[:, :256]
            sib[...] += part[:, 256:]
    for e, ref in enumerate((b0, b1, b2)):
        rows = slice(e * 224, e * 224 + 224)
        for p in range(4):
            part = lax.dot_general(ref[p], w[p, :, 512:1024], NT, preferred_element_type=F32)
            own[rows, :] += part[:, :256]
            sib[rows, :] += part[:, 256:]


def near_product(a_parts, b_parts, w):
    out = jax.ShapeDtypeStruct((896, 256), F32)
    return pl.pallas_call(
        near_kernel,
        out_shape=(out, out),
        compiler_params=params(22),
        cost_estimate=cost(12, 3),
        name="near_product",
    )(*a_parts, *b_parts, w)


def far_kernel(where, a_low, a_high, b_low, b_high, w, own_in, sib_in, own, sib):
    for e in range(4):
        at = slice(e * 224, e * 224 + 224)
        rows = pl.ds(pl.multiple_of(where[43 + e] * 224, 16), 224)
        block = (a_low, a_high)[e // 2][e % 2]
        part = lax.dot_general(block, w[3, :, 0:512], NT, preferred_element_type=F32)
        if e == 3:
            for p in range(4):
                more = (b_low, b_high)[p // 2][p % 2]
                part += lax.dot_general(more, w[p, :, 512:1024], NT, preferred_element_type=F32)
        own[rows, :] = own_in[at, :] + part[:, :256]
        sib[rows, :] = sib_in[at, :] + part[:, 256:]


def far_product(where, a_parts, b_parts, w, own, sib):
    out = jax.ShapeDtypeStruct((896, 256), F32)
    operands = (*a_parts, *b_parts, w, own, sib)
    return pl.pallas_call(
        far_kernel,
        out_shape=(out, out),
        in_specs=[SCALARS] + [whole(*operand.shape) for operand in operands],
        compiler_params=params(18),
        cost_estimate=cost(8, 1),
        name="far_product",
    )(where, *operands)


def gradient_kernel(own, other, target, scale, out):
    both = own[...] + other[...]
    gate, up = both[:, :128], both[:, 128:]
    sig = jax.nn.sigmoid(gate)
    hidden = gate * sig * up
    loss_grad = scale[...] * (hidden - target[...].astype(F32))
    grad = loss_grad * up * sig * (1.0 + gate * (1.0 - sig))
    out[...] = jnp.transpose(grad)[:112, :].astype(BF16)


def gradient(own, other, target, scale):
    return pl.pallas_call(
        gradient_kernel,
        out_shape=jax.ShapeDtypeStruct((112, 896), BF16),
        compiler_params=params(10),
        name="gradient",
    )(own, other, target, scale)


def pick_kernel(where, *refs):
    a_refs, b_refs, out = refs[0:5], refs[5:10], refs[10]
    x = where[43]

    def rows(e):
        return pl.ds(pl.multiple_of(where[43 + e] * 224, 16), 224)

    for e in range(4):
        out[rows(e), 0:512] = a_refs[0][e]
        out[rows(e), 512:1024] = b_refs[e][0]
    lanes = pl.ds(pl.multiple_of(x % 2 * 256, 256), 256)
    for p in range(4):

        @pl.when((where[17] == p) & (x < 2))
        def _():
            for e in range(4):
                ref, row = (a_refs[p], e) if p < 3 else (a_refs[3 + e // 2], e % 2)
                out[rows(e), 1024:1280] = ref[row, :, lanes]

        @pl.when((where[17] == p) & (x >= 2))
        def _():
            for e in range(4):
                ref, row = (b_refs[e], p) if e < 3 else (b_refs[3 + p // 2], p % 2)
                out[rows(e), 1024:1280] = ref[row, :, lanes]


def pick(where, a_parts, b_parts):
    operands = (*a_parts, *b_parts)
    return pl.pallas_call(
        pick_kernel,
        out_shape=jax.ShapeDtypeStruct((896, 1280), BF16),
        in_specs=[SCALARS] + [whole(*operand.shape) for operand in operands],
        compiler_params=params(14),
        cost_estimate=cost(12),
        name="pick",
    )(where, *operands)


def covariance_kernel(where, mine, other, mine_left, other_left, out, left):
    step = pl.program_id(0)

    @pl.when(step == 0)
    def _():
        keep = where[18] == where[16]
        both = jnp.where(keep, mine_left[...], other_left[...]).astype(F32)
        side = jnp.where(where[16] == 0, both[:, :128], both[:, 128:])
        left[...] = jnp.transpose(side).astype(BF16)

    right = jnp.where(step % 2 == 0, mine[...], other[...])
    tile = lax.dot_general(
        left[...], right, (((1,), (0,)), ((), ())), preferred_element_type=F32
    )
    out[...] = tile * (1.0 / 896.0)


def covariance(where, mine, other):
    chunk = (896, 256)
    return pl.pallas_call(
        covariance_kernel,
        out_shape=jax.ShapeDtypeStruct((128, 2048), F32),
        grid_spec=pltpu.PrefetchScalarGridSpec(
            num_scalar_prefetch=1,
            grid=(8,),
            in_specs=[
                pl.BlockSpec(chunk, lambda s, w: (0, s // 2)),
                pl.BlockSpec(chunk, lambda s, w: (0, s // 2)),
                pl.BlockSpec(chunk, lambda s, w: (0, 4)),
                pl.BlockSpec(chunk, lambda s, w: (0, 4)),
            ],
            out_specs=pl.BlockSpec(
                (128, 256), lambda s, w: (0, s // 2 + 4 * ((w[16] + s % 2) % 2))
            ),
            scratch_shapes=[pltpu.VMEM((128, 896), BF16)],
        ),
        compiler_params=params(8),
        cost_estimate=cost(8, 1),
        name="covariance",
    )(where, mine, other, mine, other)


UA, UB = 64, 48
TURN = (0, 4, 5, 6, 1, 2, 3, 7)
EARLY, LATE = (0, 1, 2, 4, 5), (3, 6, 7)


def tile_kernel(numbers, where, *refs):
    rows, refs = refs[0:5], refs[5:]
    count = sum(2 if number == 7 else 1 for number in numbers)
    a_refs, refs = refs[0:count], refs[count:]
    (x0, x0b, xd, xdb, xs, xsb, xf, xfb) = refs[0:8]
    out, left, right = refs[-3:]
    step = pl.program_id(0)
    core = where[16]

    def put(slot_x, who, first, value):
        base = (where[19 + slot_x] * 2 + who) * 112 + first
        right[pl.ds(pl.multiple_of(base, 16), value.shape[0]), :] = value

    @pl.when(step == 0)
    def _():
        for number, ref in enumerate(rows):
            base = where[23 + min(number, 3)] * 112 + (48 if number == 4 else 0)
            left[pl.ds(pl.multiple_of(base, 16), ref.shape[0]), :] = ref[...]

    for at, number in enumerate(numbers):

        @pl.when(step == at)
        def _():
            for e in range(4):
                mirror = (0, 2, 1, 3)[e]
                for half in range(2):
                    ref = a_refs[at]
                    if number < 4:
                        who, place = (core, 1 - core)[half], half * 4 + e
                    elif number < 7:
                        who, place = (1 - core, core)[half], half * 4 + mirror
                    elif half == 0:
                        who, place = core, e
                    else:
                        ref, who, place = a_refs[at + 1], 1 - core, mirror
                    put(e, who, 0, ref[place * UA : place * UA + UA, :])

    put(0, core, UA, x0[...])
    put(0, 1 - core, UA, x0b[...])
    put(1, core, UA, xd[...])
    put(1, 1 - core, UA, xdb[...])
    put(2, 1 - core, UA, xs[...])
    put(2, core, UA, xsb[...])
    put(3, core, UA, xf[...])
    put(3, 1 - core, UA, xfb[...])
    tile = lax.dot_general(left[...], right[...], NT, preferred_element_type=F32)
    out[...] = (tile * (1.0 / 896.0)).astype(BF16)


def tile(where, rows, a_parts, b_parts, numbers, base, before=None):
    first = pl.BlockSpec((UB, 896), lambda s, w: (w[47 + base + s], 0))
    turned = pl.BlockSpec((UB, 896), lambda s, w: (w[35 + w[47 + base + s]], 0))
    operands = [*rows, *a_parts, *b_parts]
    specs = [whole(*part.shape) for part in rows + a_parts]
    specs += [first] * 4 + [turned, turned, first, turned]
    aliases = {}
    if before is not None:
        aliases = {1 + len(operands): 0}
        operands.append(before)
        specs.append(pl.BlockSpec(memory_space=pl.ANY))
    return pl.pallas_call(
        functools.partial(tile_kernel, numbers),
        out_shape=jax.ShapeDtypeStruct((448, 7168), BF16),
        grid_spec=pltpu.PrefetchScalarGridSpec(
            num_scalar_prefetch=1,
            grid=(len(numbers),),
            in_specs=specs,
            out_specs=pl.BlockSpec((448, 896), lambda s, w: (0, w[27 + w[47 + base + s]])),
            scratch_shapes=[pltpu.VMEM((448, 896), BF16), pltpu.VMEM((896, 896), BF16)],
        ),
        input_output_aliases=aliases,
        compiler_params=params(18),
        cost_estimate=cost(2 * len(numbers), len(numbers)),
        name="tile",
    )(where, *operands)


def body(activations, gate_weight, up_weight, anchor_states, token_ids, anchor_layer, token_weight):
    z, x = lax.axis_index("z"), lax.axis_index("x")
    core, y = lax.axis_index("core"), lax.axis_index("y")

    def around(me, size, offs):
        return [(me + off) % size for off in offs]

    xs, ys = around(x, NX, OFF4), around(y, NY, OFF4)
    left_y, left_core = z // 2, z % 2
    place = sum((ys[p] == left_y) * p for p in range(4))
    side = 1 - 2 * core
    x_pair = [x, (x - side) % NX, (x + side) % NX, (x + 2) % NX]
    z_pair = [(z - side * h) % NZ for h in range(4)] + [(z + side * h) % NZ for h in (1, 2, 3)] + [(z + 4) % NZ]
    table = [0] * 16 + [core, place, left_core] + x_pair + ys + z_pair
    table += list(TURN) + xs + list(EARLY + LATE)
    where = jnp.stack([jnp.asarray(v, jnp.int32) for v in table])

    others = swap_core(activations)
    pair = jnp.where(
        core == 0, jnp.concatenate([activations, others], 0), jnp.concatenate([others, activations], 0)
    )
    half = lax.dynamic_slice_in_dim(pair, core * 1024, 1024, 1)
    reach = [pair_step(pair, "z", hop) for hop in (1, 2, 3)]
    far = pair_step(lax.dynamic_slice_in_dim(reach[1], core * 1024, 1024, 1), "z", 2)
    turned = swap_core(lax.dynamic_slice_in_dim(jnp.stack(reach), (1 - core) * 1024, 1024, 2))
    line = lineup(where, half, *reach, turned, far).reshape(224, 1024)

    gate_t, up_t = gate_weight.T, up_weight.T
    theirs = swap_core(away_half(where, gate_t, up_t))

    def gather(block, axis):
        parts = flat(ring(block, axis, 4, 112), OFF4)
        return join([(part, 0, part.shape[0]) for part in parts]).reshape(4, 224, 512)

    a_near, b_near = gather(line[:, :512], "x"), gather(line[:, 512:], "y")
    a_near, b_near, theirs, token_ids, anchor_layer = lax.optimization_barrier(
        (a_near, b_near, theirs, token_ids, anchor_layer)
    )
    weights = pack_weights(where, gate_t, up_t, theirs)

    def reorder(ids):
        return ids.reshape(NZ, NX, 28).transpose(1, 0, 2).reshape(896)

    padded = jnp.pad(anchor_states, ((0, 0), (0, 16)))
    target = padded[reorder(anchor_layer)]
    scale = jnp.broadcast_to(token_weight[reorder(token_ids)][:, None], (896, 128))

    a_up, a_down = shift(a_near, "y", NY, 1), shift(a_near, "y", NY, -1)
    b_up, b_down = shift(b_near, "x", NX, 1), shift(b_near, "x", NX, -1)
    b_up, b_down, weights, target, scale = lax.optimization_barrier(
        (b_up, b_down, weights, target, scale)
    )
    a_parts = [a_near, a_up, a_down, shift(a_up[:2], "y", NY, 1), shift(a_down[2:], "y", NY, -1)]
    b_parts = [b_near, b_up, b_down, shift(b_up[:2], "x", NX, 1), shift(b_down[2:], "x", NX, -1)]
    own, sib = near_product(a_parts[:3], b_parts[:3], weights)
    own, sib = far_product(where, a_parts[3:], b_parts[3:], weights, own, sib)
    grads = gradient(own, swap_core(sib), target, scale)

    mates = swap_core(grads)
    mates, grads, where_late = lax.optimization_barrier((mates, grads, where))
    chunks = pick(where_late, a_parts, b_parts)
    both = jnp.concatenate([grads[UA:], mates[UA:]], 0)
    z_near = [pair_step(both, "z", hop) for hop in (1, 2, 3)]
    x_near = pair_step(jnp.concatenate([grads[:UA], mates[:UA]], 0), "x", 1)
    x_near, chunks = lax.optimization_barrier((x_near, chunks))
    x_far, z_far = pair_step(x_near[:UA], "x", 1), pair_step(z_near[1][:UB], "z", 2)
    x_turned, x_last = swap_core(x_near), swap_core(x_far)
    by_x = join(
        [(grads, 0, UA), (x_near, 0, UA), (x_turned, UA, UA), (x_far, 0, UA)]
        + [(mates, 0, UA), (x_near, UA, UA), (x_turned, 0, UA), (x_last, 0, UA)]
    )
    z_turned, z_last = [swap_core(block) for block in z_near], swap_core(z_far)
    mine = join([(grads, UA, UB)] + [(b, 0, UB) for b in z_near] + [(b, UB, UB) for b in z_turned] + [(z_far, 0, UB)])
    others = join([(mates, UA, UB)] + [(b, UB, UB) for b in z_near] + [(b, 0, UB) for b in z_turned] + [(z_last, 0, UB)])

    hold = lax.optimization_barrier
    by_x, mine, others, grads, chunks = hold((by_x, mine, others, grads, chunks))
    z_one, x_one, chunks_b = pair_step(by_x, "z", 1), pair_step(mine, "x", 1), swap_core(chunks)
    y_up, y_down = shift(grads, "y", NY, 1), shift(grads, "y", NY, -1)
    z_one, x_one, others, y_up, y_down, chunks_b = hold((z_one, x_one, others, y_up, y_down, chunks_b))

    z_two, x_more = pair_step(z_one, "z", 1), pair_step(others, "x", 1)
    z_one_b, x_one_b = swap_core(z_one), swap_core(x_one)
    y_high = shift(y_down[48:], "y", NY, -1)
    act_covariance = covariance(where, chunks, chunks_b)
    z_two, x_more, x_one, z_one_b, x_one_b, y_up, y_high, act_covariance = hold(
        (z_two, x_more, x_one, z_one_b, x_one_b, y_up, y_high, act_covariance)
    )
    z_three, x_two = pair_step(z_two, "z", 1), pair_step(x_one, "x", 1)
    z_two_b, x_more_b = swap_core(z_two), swap_core(x_more)
    y_low = shift(y_up[:48], "y", NY, 1)
    z_three, x_two, z_two_b, x_more_b, y_low = hold((z_three, x_two, z_two_b, x_more_b, y_low))

    z_four = pair_step(z_three[: 4 * UA], "z", 1)
    z_three_b, x_two_b = swap_core(z_three), swap_core(x_two)
    rows = [grads, y_up, y_down, y_low, y_high]
    x_all = [mine, others, x_one, x_more, x_one_b, x_more_b, x_two, x_two_b]
    columns = tile(where, rows, [by_x, z_one, z_two, z_one_b, z_two_b], x_all, EARLY, 0)
    z_four, columns = hold((z_four, columns))
    late = [z_three, z_three_b, z_four, swap_core(z_four)]
    return act_covariance, tile(where, rows, late, x_all, LATE, len(EARLY), columns)


def solution(mesh):
    fine = Mesh(mesh.devices.reshape(NZ, NX, NC, NY), ("z", "x", "core", "y"))
    dp = ("z", "x", "core")
    units = P(None, dp + ("y",))
    in_specs = (P(dp, "y"), units, units, units, P(), P(), P())
    out_specs = (P(dp, "y"), P(dp, "y"))
    return jax.shard_map(body, mesh=fine, in_specs=in_specs, out_specs=out_specs, check_vma=False)
```
